128 devices in a mesh: lat: 32 (over x, y, core), ch: 4 (over z).
Axes of the slice: x: 4, y: 4, z: 4, core: 2. Of those that a mesh axis runs over, the one named last changes fastest.
Arguments:
- state: float32 [128, 256, 1024], P('lat', None, 'ch'), may hold values from -6 to 6
- residual: float32 [128, 256, 1024], P('lat', None, 'ch'), may hold values from -6 to 6
- direction: float32 [128, 256, 1024], P('lat', None, 'ch'), may hold values from -6 to 6
- precond: float32 [128, 256, 1024], P('lat', None, 'ch'), may hold values from 0.5 to 4
- token_slope: bfloat16 [32768, 4096], P('lat', 'ch'), may hold values from -0.099609375 to 1.09375
- spectral_slope: bfloat16 [2, 128, 128, 1024], P(None, None, 'lat', 'ch'), may hold values from -0.099609375 to 1.09375
- filter_in: float32 [2, 8, 128, 128], P(None, 'ch'), may hold values from -0.375 to 0.375
- filter_out: float32 [2, 8, 128, 128], P(None, 'ch'), may hold values from -0.375 to 0.375
- w_up: bfloat16 [1024, 4096], P(None, 'ch'), may hold values from -0.1875 to 0.1875
- w_down: bfloat16 [4096, 1024], P('ch'), may hold values from -0.09375 to 0.09375
- obs_weight: float32 [1024], P('ch'), may hold values from -0.6 to 0.6
- obs_token: int32 [32, 4, 128], P('lat'), may hold values from 0 to 32767
- obs_count: int32 [32, 4], P('lat'), may hold values from 1 to 128, 320 in all within a row
- obs_rinv: float32 [32, 4, 128], P('lat'), may hold values from 1 to 10
Outputs:
- state_next: float32 [128, 256, 1024], P('lat', None, 'ch')
- residual_next: float32 [128, 256, 1024], P('lat', None, 'ch')
- direction_next: float32 [128, 256, 1024], P('lat', None, 'ch')
The draws below stay inside these ranges and needn't reach their ends.
Inputs may be any that keep to these rules, and one draw needn't show every extreme that they name: `obs_count`: in every latitude band the 4 counts sum to 320, and the largest is 128.
All inputs are finite; a program needn't handle non-finite values.
Results may differ from the reference program's by a relative error of at most 0.015.
Values may be sent and summed in bfloat16 or wider, within the bound.
A program may use at most 128 MiB of HBM per device.

```python
import math
import jax
import jax.numpy as jnp
import numpy as np
from jax import lax

W = 256
D = 1024
FF = 4096
BS = 128
BLK_DEV = 4
OB = 128
NB = 8
H = 128
KW = 128
TOKENS = 32768
OBS_BAND = 320
N_LAT = 32


def with_ends(array, rng, smallest, high):
    longest = array.shape.index(max(array.shape))
    spots = []
    for shift in (0, 1):
        where = [jax.random.randint(jax.random.fold_in(rng, axis), (), 0, length) for axis, length in enumerate(array.shape)]
        where[longest] = (where[longest] + shift) % array.shape[longest]
        spots.append(tuple(where))
    return array.at[spots[0]].set(smallest).at[spots[1]].set(high)


def shard_levels(stream_key, shape, shards, least, high):
    gain, own = 1.0, jax.random.fold_in(stream_key, 6)
    for dim, blocks in shards:
        heights = jnp.exp(jax.random.uniform(jax.random.fold_in(own, dim), (blocks,), jnp.float32, least / len(shards), high / len(shards)))
        gain = gain * jnp.repeat(heights, shape[dim] // blocks).reshape([-1 if axis == dim else 1 for axis in range(len(shape))])
    return gain


def profile(count, total, reach, skew):
    portions = [(1 << 20) // math.isqrt(rank ** skew) + 1 for rank in range(2, count + 1)]
    surplus, given = total - reach - (count - 1), [1] * (count - 1)
    while surplus > 0:
        movable = [i for i in range(count - 1) if given[i] < reach]
        mass, left = sum([portions[i] for i in movable]), surplus
        for i in movable:
            extra = min(reach - given[i], max(1, left * portions[i] // mass), surplus)
            given[i] = given[i] + extra
            surplus = surplus - extra
    return np.array([reach] + given)


def uneven_parts(own_key, count, total, limit, skew):
    if count == 2:
        one = jax.random.randint(own_key, (), max(1, total - limit), min(limit, total - 1) + 1)
        return jnp.stack([one, total - one])
    tallies = jnp.asarray(profile(count, total, limit, skew), jnp.int32)
    twos = (count - 1) // 2
    giver, taker = tallies[1:1 + 2 * twos:2], tallies[2:2 + 2 * twos:2]
    slack = jnp.minimum(giver - 1, limit - taker)
    moved = jax.random.randint(jax.random.fold_in(own_key, 1), (twos,), 0, 1 << 20) % (slack + 1)
    tallies = tallies.at[1:1 + 2 * twos:2].set(giver - moved).at[2:2 + 2 * twos:2].set(taker + moved)
    return tallies[jax.random.permutation(jax.random.fold_in(own_key, 2), count)]


def noise(rng, extent, scale, most, shards=(), kind=jnp.bfloat16):
    gain = shard_levels(rng, extent, shards, -0.22, 0.18) if shards else 1.0
    result = jax.random.normal(rng, extent, jnp.float32) * scale * gain
    return jnp.minimum(jnp.maximum(result, -most), most).astype(kind)


def setup_inputs(seed: int = 0) -> dict:
    keys = jax.random.split(jax.random.key(seed), 15)
    return {
        "state": noise(keys[0], (H, W, D), 1.0, 6.0, ((0, 32), (2, 4)), jnp.float32),
        "residual": noise(keys[1], (H, W, D), 1.0, 6.0, ((0, 32), (2, 4)), jnp.float32),
        "direction": noise(keys[2], (H, W, D), 1.0, 6.0, ((0, 32), (2, 4)), jnp.float32),
        "precond": jnp.clip(jnp.exp(math.log(4.0) - 2.0794415 * jax.random.uniform(keys[3], (H, W, D), jnp.float32) ** shard_levels(keys[3], (H, W, D), ((0, 32), (2, 4)), -0.2, 0.2)), 0.5, 4.0),
        "token_slope": jnp.clip(-0.099609375 + 1.1933594 * jax.random.uniform(keys[4], (TOKENS, FF), jnp.float32) ** shard_levels(keys[4], (TOKENS, FF), ((0, 32), (1, 4)), -0.2, 0.2), -0.099609375, 1.09375).astype(jnp.bfloat16),
        "spectral_slope": jnp.clip(-0.099609375 + 1.1933594 * jax.random.uniform(keys[5], (2, H, KW, D), jnp.float32) ** shard_levels(keys[5], (2, H, KW, D), ((2, 32), (3, 4)), -0.2, 0.2), -0.099609375, 1.09375).astype(jnp.bfloat16),
        "filter_in": noise(keys[6], (2, NB, BS, BS), (2 * BS) ** -0.5, 0.375, ((1, 4),), jnp.float32),
        "filter_out": noise(keys[7], (2, NB, BS, BS), (2 * BS) ** -0.5, 0.375, ((1, 4),), jnp.float32),
        "w_up": noise(keys[8], (D, FF), D ** -0.5, 0.1875, ((1, 4),)),
        "w_down": noise(keys[9], (FF, D), FF ** -0.5, 0.09375, ((0, 4),)),
        "obs_weight": noise(keys[10], (D,), 0.1, 0.6, ((0, 4),), jnp.float32),
        "obs_token": with_ends(jax.random.randint(keys[11], (N_LAT, BLK_DEV, OB), 0, H * W), jax.random.fold_in(keys[11], 1), 0, (H * W) - 1).astype(jnp.int32),
        "obs_count": jax.vmap(lambda own: uneven_parts(own, BLK_DEV, OBS_BAND, OB, 2))(jax.random.split(keys[12], N_LAT)).reshape((N_LAT, BLK_DEV)).astype(jnp.int32),
        "obs_rinv": jnp.clip(jnp.exp(math.log(10.0) - 2.3025851 * jax.random.uniform(keys[13], (N_LAT, BLK_DEV, OB), jnp.float32) ** shard_levels(keys[13], (N_LAT, BLK_DEV, OB), ((0, 32),), -0.2, 0.2)), 1.0, 10.0),
    }


HIGH = lax.Precision.HIGHEST


def tables(length, count):
    freq = lax.broadcasted_iota(jnp.int32, (count, length), 0)
    place = lax.broadcasted_iota(jnp.int32, (count, length), 1)
    angle = (2.0 * math.pi / length) * ((freq * place) % length).astype(jnp.float32)
    return jnp.cos(angle), jnp.sin(angle)


def spectral_tables(width, height):
    lon_cos, lon_sin = tables(width, width // 2)
    wave = lax.broadcasted_iota(jnp.int32, (width // 2, 1), 0)
    factor = jnp.where(wave == 0, jnp.float32(1.0), jnp.float32(2.0)) / width
    lat_cos, lat_sin = tables(height, height)
    return lon_cos, lon_sin, lon_cos * factor, lon_sin * factor, lat_cos, lat_sin


def lon_forward(field, cos_table, sin_table):
    real_part = jnp.einsum("kw,lwd->lkd", cos_table, field, precision=HIGH)
    imag_part = -jnp.einsum("kw,lwd->lkd", sin_table, field, precision=HIGH)
    return real_part, imag_part


def lon_backward(real_part, imag_part, cos_table, sin_table):
    first_term = jnp.einsum("kw,lkd->lwd", cos_table, real_part, precision=HIGH)
    return first_term - jnp.einsum("kw,lkd->lwd", sin_table, imag_part, precision=HIGH)


def lat_mix(real_part, imag_part, cos_table, sin_table, sign):
    cos_real = jnp.einsum("mh,hkd->mkd", cos_table, real_part, precision=HIGH)
    cos_imag = jnp.einsum("mh,hkd->mkd", cos_table, imag_part, precision=HIGH)
    sin_real = jnp.einsum("mh,hkd->mkd", sin_table, real_part, precision=HIGH)
    sin_imag = jnp.einsum("mh,hkd->mkd", sin_table, imag_part, precision=HIGH)
    return cos_real + sign * sin_imag, cos_imag - sign * sin_real


def block_product(real_part, imag_part, weights, flip):
    lead = real_part.shape[:-1]
    blocks = weights.shape[1]
    width = weights.shape[2]
    real_blocks = real_part.reshape(lead + (blocks, width))
    imag_blocks = imag_part.reshape(lead + (blocks, width))
    if flip:
        form = "hknc,nbc->hknb"
        other = -weights[1]
    else:
        form = "hknb,nbc->hknc"
        other = weights[1]
    new_real = jnp.einsum(form, real_blocks, weights[0], precision=HIGH) - jnp.einsum(form, imag_blocks, other, precision=HIGH)
    new_imag = jnp.einsum(form, real_blocks, other, precision=HIGH) + jnp.einsum(form, imag_blocks, weights[0], precision=HIGH)
    return new_real.reshape(lead + (blocks * width,)), new_imag.reshape(lead + (blocks * width,))


def spectral(field, slope, first, second, tabs, flip):
    lon_cos, lon_sin, inv_cos, inv_sin, lat_cos, lat_sin = tabs
    height = lat_cos.shape[0]
    if flip:
        real_part, imag_part = lon_forward(field, inv_cos, inv_sin)
        real_part, imag_part = lat_mix(real_part, imag_part, lat_cos / height, lat_sin / height, 1.0)
    else:
        real_part, imag_part = lon_forward(field, lon_cos, lon_sin)
        real_part, imag_part = lat_mix(real_part, imag_part, lat_cos, lat_sin, 1.0)
    real_part, imag_part = block_product(real_part, imag_part, first, flip)
    real_part = real_part * slope[0].astype(jnp.float32)
    imag_part = imag_part * slope[1].astype(jnp.float32)
    real_part, imag_part = block_product(real_part, imag_part, second, flip)
    if flip:
        real_part, imag_part = lat_mix(real_part, imag_part, lat_cos, lat_sin, -1.0)
        return lon_backward(real_part, imag_part, lon_cos, lon_sin)
    real_part, imag_part = lat_mix(real_part, imag_part, lat_cos / height, lat_sin / height, -1.0)
    return lon_backward(real_part, imag_part, inv_cos, inv_sin)


def product(left, right, flip):
    if flip:
        return lax.dot_general(left, right, (((1,), (1,)), ((), ())), preferred_element_type=jnp.float32)
    return jnp.dot(left, right, preferred_element_type=jnp.float32)


def mix_rows(rows, first, second, slope, flip):
    hidden = (product(rows.astype(jnp.bfloat16), first, flip) * slope).astype(jnp.bfloat16)
    return product(hidden, second, flip)


def token_mix(field, first, second, slope, flip):
    height, width, depth = field.shape
    slopes = slope.reshape(height, width, slope.shape[1])

    def one_band(pair):
        return mix_rows(pair[0], first, second, pair[1], flip)

    return lax.map(one_band, (field, slopes))


def reference(state, residual, direction, precond, token_slope, spectral_slope, filter_in, filter_out, w_up, w_down, obs_weight, obs_token, obs_count, obs_rinv):
    tabs = spectral_tables(W, H)
    first = direction + spectral(direction, spectral_slope, filter_in, filter_out, tabs, False)
    second = first + token_mix(first, w_up, w_down, token_slope, False)
    projected = jnp.dot(second.reshape(H * W, D), obs_weight, precision=HIGH)
    picked = projected[obs_token]
    slots = lax.broadcasted_iota(jnp.int32, obs_token.shape, 2)
    weighted = jnp.where(slots < obs_count[:, :, None], obs_rinv * picked, jnp.float32(0.0))
    gathered = jnp.zeros((H * W,), jnp.float32).at[obs_token.reshape(-1)].add(weighted.reshape(-1))
    back_field = (gathered[:, None] * obs_weight[None, :]).reshape(H, W, D)
    back_mid = back_field + token_mix(back_field, w_down, w_up, token_slope, True)
    image = direction + back_mid + spectral(back_mid, spectral_slope, filter_out, filter_in, tabs, True)
    norm_now = jnp.sum(residual * residual / precond)
    curve = jnp.sum(direction * image)
    alpha = norm_now / curve
    state_next = state + alpha * direction
    residual_next = residual - alpha * image
    scaled = residual_next / precond
    norm_next = jnp.sum(residual_next * scaled)
    direction_next = scaled + (norm_next / norm_now) * direction
    return state_next, residual_next, direction_next
```

```python
import math

import jax
import jax.numpy as jnp
from jax import lax
from jax.sharding import PartitionSpec as P

HIGH = lax.Precision.HIGHEST


def tables(length, count):
    freq = lax.broadcasted_iota(jnp.int32, (count, length), 0)
    place = lax.broadcasted_iota(jnp.int32, (count, length), 1)
    angle = 2.0 * math.pi / length * (freq * place % length).astype(jnp.float32)
    return (jnp.cos(angle), jnp.sin(angle))


def spectral_tables(width, height):
    lon_cos, lon_sin = tables(width, width // 2)
    wave = lax.broadcasted_iota(jnp.int32, (width // 2, 1), 0)
    factor = jnp.where(wave == 0, jnp.float32(1.0), jnp.float32(2.0)) / width
    lat_cos, lat_sin = tables(height, height)
    return (lon_cos, lon_sin, lon_cos * factor, lon_sin * factor, lat_cos, lat_sin)


def lon_forward(field, cos_table, sin_table):
    real_part = jnp.einsum("kw,lwd->lkd", cos_table, field, precision=HIGH)
    imag_part = -jnp.einsum("kw,lwd->lkd", sin_table, field, precision=HIGH)
    return (real_part, imag_part)


def lon_backward(real_part, imag_part, cos_table, sin_table):
    first_term = jnp.einsum("kw,lkd->lwd", cos_table, real_part, precision=HIGH)
    return first_term - jnp.einsum("kw,lkd->lwd", sin_table, imag_part, precision=HIGH)


def lat_mix(real_part, imag_part, cos_table, sin_table, sign):
    cos_real = jnp.einsum("mh,hkd->mkd", cos_table, real_part, precision=HIGH)
    cos_imag = jnp.einsum("mh,hkd->mkd", cos_table, imag_part, precision=HIGH)
    sin_real = jnp.einsum("mh,hkd->mkd", sin_table, real_part, precision=HIGH)
    sin_imag = jnp.einsum("mh,hkd->mkd", sin_table, imag_part, precision=HIGH)
    return (cos_real + sign * sin_imag, cos_imag - sign * sin_real)


def block_product(real_part, imag_part, weights, flip):
    lead = real_part.shape[:-1]
    blocks = weights.shape[1]
    width = weights.shape[2]
    real_blocks = real_part.reshape(lead + (blocks, width))
    imag_blocks = imag_part.reshape(lead + (blocks, width))
    if flip:
        form = "hknc,nbc->hknb"
        other = -weights[1]
    else:
        form = "hknb,nbc->hknc"
        other = weights[1]
    new_real = jnp.einsum(form, real_blocks, weights[0], precision=HIGH) - jnp.einsum(
        form, imag_blocks, other, precision=HIGH
    )
    new_imag = jnp.einsum(form, real_blocks, other, precision=HIGH) + jnp.einsum(
        form, imag_blocks, weights[0], precision=HIGH
    )
    return (new_real.reshape(lead + (blocks * width,)), new_imag.reshape(lead + (blocks * width,)))


def spectral(field, slope, first, second, tabs, flip):
    lon_cos, lon_sin, inv_cos, inv_sin, lat_cos, lat_sin = tabs
    if flip:
        real_part, imag_part = lon_forward(field, inv_cos, inv_sin)
    else:
        real_part, imag_part = lon_forward(field, lon_cos, lon_sin)
    real_part, imag_part = (
        lax.all_to_all(
            real_part.astype(jnp.bfloat16), "lat", split_axis=1, concat_axis=0, tiled=True
        ).astype(real_part.dtype),
        lax.all_to_all(
            imag_part.astype(jnp.bfloat16), "lat", split_axis=1, concat_axis=0, tiled=True
        ).astype(imag_part.dtype),
    )
    height = lat_cos.shape[0]
    if flip:
        real_part, imag_part = lat_mix(
            real_part, imag_part, lat_cos / height, lat_sin / height, 1.0
        )
    else:
        real_part, imag_part = lat_mix(real_part, imag_part, lat_cos, lat_sin, 1.0)
    real_part, imag_part = block_product(real_part, imag_part, first, flip)
    real_part = real_part * slope[0].astype(jnp.float32)
    imag_part = imag_part * slope[1].astype(jnp.float32)
    real_part, imag_part = block_product(real_part, imag_part, second, flip)
    if flip:
        real_part, imag_part = lat_mix(real_part, imag_part, lat_cos, lat_sin, -1.0)
    else:
        real_part, imag_part = lat_mix(
            real_part, imag_part, lat_cos / height, lat_sin / height, -1.0
        )
    real_part, imag_part = (
        lax.all_to_all(
            real_part.astype(jnp.bfloat16), "lat", split_axis=0, concat_axis=1, tiled=True
        ).astype(real_part.dtype),
        lax.all_to_all(
            imag_part.astype(jnp.bfloat16), "lat", split_axis=0, concat_axis=1, tiled=True
        ).astype(imag_part.dtype),
    )
    if flip:
        return lon_backward(real_part, imag_part, lon_cos, lon_sin)
    return lon_backward(real_part, imag_part, inv_cos, inv_sin)


def product(left, right, flip):
    if flip:
        return lax.dot_general(
            left, right, (((1,), (1,)), ((), ())), preferred_element_type=jnp.float32
        )
    return jnp.dot(left, right, preferred_element_type=jnp.float32)


def shards(
    state,
    residual,
    direction,
    precond,
    token_slope,
    spectral_slope,
    filter_in,
    filter_out,
    w_up,
    w_down,
    obs_weight,
    obs_token,
    obs_count,
    obs_rinv,
):
    bands, width, depth = direction.shape
    height = bands * lax.axis_size("lat")
    tabs = spectral_tables(width, height)
    own_now = jnp.sum(residual * residual / precond)
    own_square = jnp.sum(direction * direction)

    slots = lax.broadcasted_iota(jnp.int32, obs_token.shape, 2)
    live = jnp.where(slots < obs_count[:, :, None], obs_rinv, jnp.float32(0.0))
    spread = jnp.zeros((height * width,), jnp.float32).at[obs_token.reshape(-1)].add(live.reshape(-1))
    rsum = lax.psum_scatter(spread, "lat", scatter_dimension=0, tiled=True)

    whole_weight = lax.all_gather(obs_weight, "ch", axis=0, tiled=True)
    up = jnp.dot(w_down.astype(jnp.float32), whole_weight, precision=HIGH)
    scaled_slope = (token_slope * up[None, :]).astype(jnp.bfloat16)
    partial_q = product(scaled_slope, w_up, True)
    q = lax.psum_scatter(partial_q.astype(jnp.bfloat16), "ch", scatter_dimension=1, tiled=True)
    q = q.astype(jnp.float32) + obs_weight[None, :]

    first = direction + spectral(direction, spectral_slope, filter_in, filter_out, tabs, False)
    first_rows = first.reshape(bands * width, depth)
    projected = lax.psum(jnp.sum(first_rows * q, axis=1), "ch")
    back_rows = rsum * projected
    own_curve = own_square + jnp.sum(back_rows * projected) / lax.axis_size("ch")
    sums = lax.psum(jnp.stack([own_now, own_curve]), ("lat", "ch"))
    norm_now, curve = sums[0], sums[1]
    back_mid = (back_rows[:, None] * q).reshape(bands, width, depth)
    image = (
        direction + back_mid + spectral(back_mid, spectral_slope, filter_out, filter_in, tabs, True)
    )
    alpha = norm_now / curve
    state_next = state + alpha * direction
    residual_next = residual - alpha * image
    scaled = residual_next / precond
    norm_next = lax.psum(jnp.sum(residual_next * scaled), ("lat", "ch"))
    direction_next = scaled + norm_next / norm_now * direction
    return (state_next, residual_next, direction_next)


def solution(mesh):
    return jax.shard_map(
        shards,
        mesh=mesh,
        in_specs=(
            P("lat", None, "ch"),
            P("lat", None, "ch"),
            P("lat", None, "ch"),
            P("lat", None, "ch"),
            P("lat", "ch"),
            P(None, None, "lat", "ch"),
            P(None, "ch", None, None),
            P(None, "ch", None, None),
            P(None, "ch"),
            P("ch", None),
            P("ch"),
            P("lat", None, None),
            P("lat", None),
            P("lat", None, None),
        ),
        out_specs=(P("lat", None, "ch"), P("lat", None, "ch"), P("lat", None, "ch")),
        check_vma=False,
    )
```

```python
import functools
import math

import jax
import jax.numpy as jnp
import ml_dtypes
import numpy as np
from jax import lax
from jax.experimental import pallas as pl
from jax.experimental.pallas import tpu as pltpu
from jax.sharding import PartitionSpec as P

MESH = pl.DeviceIdType.MESH
F32 = jnp.float32
BF = jnp.bfloat16
NT = (((1,), (1,)), ((), ()))
N_LAT = 32
N_CH = 4


def halves(table):
    high = table.astype(ml_dtypes.bfloat16)
    low = (table - high.astype(np.float32)).astype(ml_dtypes.bfloat16)
    return high, low


def angles(length, count):
    place = (np.arange(count)[:, None] * np.arange(length)[None, :]) % length
    angle = (2.0 * math.pi / length) * place.astype(np.float64)
    return np.cos(angle).astype(np.float32), np.sin(angle).astype(np.float32)


def make_tables(width, height):
    count = width // 2
    cos, sin = angles(width, count)
    scale = np.where(np.arange(count) == 0, 1.0, 2.0).astype(np.float32)[:, None] / width
    per = count // N_LAT

    def spectral_rows(c, s):
        both = np.stack([c.reshape(N_LAT, per, width), -s.reshape(N_LAT, per, width)], axis=1)
        return both.reshape(2 * count, width).astype(np.float32)

    plain = spectral_rows(cos, sin)
    inverse = spectral_rows(cos * scale, sin * scale)
    lat_cos, lat_sin = angles(height, height)
    mix = np.zeros((2, height, height, 2), np.float32)
    mix[0, :, :, 0] = lat_cos
    mix[0, :, :, 1] = lat_sin
    mix[1, :, :, 0] = -lat_sin
    mix[1, :, :, 1] = lat_cos
    mix = mix.reshape(2 * height, 2 * height)
    unmix = np.ascontiguousarray(mix.T) / np.float32(height)

    def left(table, parts):
        high, low = halves(np.ascontiguousarray(table))
        return np.concatenate([high, low, high][:parts], axis=1)

    return dict(
        lon=left(plain, 3),
        back=left(inverse.T, 2),
        lon_adj=inverse,
        back_adj=left(plain.T, 2),
        mix=left(mix, 2),
        unmix=left(unmix, 3),
    )


def split(x):
    high = x.astype(BF)
    return high, (x - high.astype(F32)).astype(BF)


def dot(a, b):
    return jnp.dot(a, b, preferred_element_type=F32)


def dot_nt(a, b):
    return lax.dot_general(a, b, NT, preferred_element_type=F32)


def right3(x):
    high, low = split(x)
    return jnp.concatenate([high, high, low], axis=0)


def left3(x):
    high, low = split(x)
    return jnp.concatenate([high, low, high], axis=1)


def kernel(
    count_ref, d_hbm, r_hbm, p_hbm, slope_hbm, sslope_hbm, fin_hbm, fout_hbm, wup_hbm, wdown_hbm,
    ow_hbm, tok_hbm, rinv_hbm, lon_hbm, back_hbm, lona_hbm, backa_hbm, mix_hbm, unmix_hbm,
    rn_hbm, scal_ref,
    d, r, p, slope, sslope, fin, fout, wup, wdown, tok, rinv, lon_t, back_t, lona_t, backa_t,
    mix_t, unmix_t, owz, sl, wk, wl, wupu, g_far, g_own, g_next, g_prev, q, qcat, esum, base,
    spread, lat_rows, send, recv, rpart, rrecv, out_far, out_next, out_prev, out_acc,
    in_far, in_next, in_prev, in_acc, proj, ar1, ar1z, ar2, ar2z, rn,
    load_sem, a_send, a_recv, z_send, z_recv, s_send, s_recv, out_sem,
):
    me = lax.axis_index("lat")
    z = lax.axis_index("ch")
    px, py, pc = me // 8, (me // 2) % 4, me % 2
    z_next, z_prev, z_far = (z + 1) % 4, (z + 3) % 4, (z + 2) % 4

    def peer(o):
        dx, dy, dc = o // 8, (o // 2) % 4, o % 2
        return ((px + dx) % 4) * 8 + ((py + dy) % 4) * 2 + (pc + dc) % 2

    loads = [
        pltpu.make_async_copy(src, dst, load_sem.at[i])
        for i, (src, dst) in enumerate([
            (d_hbm, d), (lon_hbm, lon_t), (tok_hbm, tok), (rinv_hbm, rinv), (ow_hbm, owz.at[z]),
            (wdown_hbm, wdown), (wup_hbm, wup), (slope_hbm, slope), (mix_hbm, mix_t), (fin_hbm, fin),
            (fout_hbm, fout), (sslope_hbm, sslope), (unmix_hbm, unmix_t), (back_hbm, back_t),
            (r_hbm, r), (p_hbm, p), (lona_hbm, lona_t), (backa_hbm, backa_t),
        ])
    ]
    for copy in loads:
        copy.start()
    (l_d, l_lon, l_tok, l_rinv, l_ow, l_wdown, l_wup, l_slope, l_mix, l_fin, l_fout, l_sslope,
     l_unmix, l_back, l_r, l_p, l_lona, l_backa) = loads

    barrier = pltpu.get_barrier_semaphore()

    def greet(o, carry):
        pl.semaphore_signal(barrier, inc=1, device_id=(peer(o), z), device_id_type=MESH)
        return carry

    lax.fori_loop(1, N_LAT, greet, 0)
    for other in (z_next, z_prev, z_far):
        pl.semaphore_signal(barrier, inc=1, device_id=(me, other), device_id_type=MESH)

    def to_all(src_of, dst, send_sem, recv_sem):
        def go(o, carry):
            other = peer(o)
            pltpu.make_async_remote_copy(
                src_of(other), dst, send_sem, recv_sem, device_id=(other, z), device_id_type=MESH
            ).start()
            return carry

        lax.fori_loop(1, N_LAT, go, 0)

    def wait_for(ref, n, sem):
        part = ref.at[pl.ds(0, n)]
        pltpu.make_async_copy(part, part, sem).wait()

    def scatter(stage, c):
        i = stage * 2 + c
        recv[i, me] = send[i, me]
        to_all(lambda o: send.at[i, o], recv.at[i, me], a_send.at[i], a_recv.at[i])

    def arrive(stage, c):
        i = stage * 2 + c
        wait_for(recv.at[i], N_LAT - 1, a_recv.at[i])
        return recv[i]

    def z_copy(src, dst, other, k):
        copy = pltpu.make_async_remote_copy(
            src, dst, z_send.at[k], z_recv.at[k], device_id=(me, other), device_id_type=MESH
        )
        copy.start()
        return copy

    def pack_rows(stage, c, out):
        rows = out.reshape(N_LAT, 8, 512)
        rows = jnp.concatenate([rows[:, :, 128 * h:128 * h + 128] for h in range(4)], axis=1)
        send[stage * 2 + c] = rows.astype(BF)

    l_d.wait()
    l_lon.wait()
    for c in range(2):
        x = jnp.concatenate([d[h, :, 128 * c:128 * c + 128] for h in range(4)], axis=1)
        pack_rows(0, c, dot(lon_t[...], right3(x)))

    l_tok.wait()
    l_rinv.wait()
    where_high, where_low = [], []
    rows_high = lax.broadcasted_iota(jnp.int32, (256, 128), 0)
    rows_low = lax.broadcasted_iota(jnp.int32, (128, 128), 0)
    lane = lax.broadcasted_iota(jnp.int32, (1, 128), 1)
    for j in range(4):
        token = tok[0, j:j + 1, :]
        live = jnp.where(lane < count_ref[0, j], rinv[0, j:j + 1, :], 0.0)
        hot = jnp.where(rows_high == (token >> 7), 1.0, 0.0).astype(BF)
        value = jnp.where(rows_low == (token & 127), live, 0.0)
        v0, rest = value.astype(BF), value - value.astype(BF).astype(F32)
        v1, v2 = split(rest)
        where_high += [hot, hot, hot]
        where_low += [v0, v1, v2]
    spread_now = dot_nt(jnp.concatenate(where_high, axis=1), jnp.concatenate(where_low, axis=1))
    rpart[...] = spread_now.reshape(N_LAT, 8, 128)

    l_ow.wait()
    pl.semaphore_wait(barrier, N_LAT - 1 + N_CH - 1)

    ow_copies = [
        pltpu.make_async_remote_copy(
            owz.at[z], owz.at[z], s_send.at[0], s_recv.at[0], device_id=(me, other),
            device_id_type=MESH)
        for other in (z_next, z_prev, z_far)
    ]
    for copy in ow_copies:
        copy.start()
    scatter(0, 0)
    scatter(0, 1)
    rrecv[me] = rpart[me]
    to_all(lambda o: rpart.at[o], rrecv.at[me], s_send.at[1], s_recv.at[1])

    l_wdown.wait()
    l_wup.wait()
    l_slope.wait()
    wait_for(owz, 3, s_recv.at[0])
    weight = jnp.concatenate([owz[j] for j in range(4)], axis=1)
    w0, rest = weight.astype(BF), weight - weight.astype(BF).astype(F32)
    w1, w2 = split(rest)
    sub = lax.broadcasted_iota(jnp.int32, (8, 1024), 0)
    zero = jnp.zeros((8, 1024), F32)
    parts = jnp.where(sub == 0, w0.astype(F32), jnp.where(sub == 1, w1.astype(F32), jnp.where(
        sub == 2, w2.astype(F32), zero)))
    u = jnp.sum(dot_nt(parts.astype(BF), wdown[...]), axis=0, keepdims=True)
    wupu[...] = (wup[...].astype(F32) * u).astype(BF)

    def share(owner, dst):
        cols = wupu[pl.ds(pl.multiple_of(owner * 256, 256), 256), :]

        def rows(i, carry):
            at = pl.ds(pl.multiple_of(i * 256, 256), 256)
            dst[at, :] = dot_nt(slope[at, :], cols).astype(dst.dtype)
            return carry

        lax.fori_loop(0, 4, rows, 0)

    top, low = pl.ds(0, 512), pl.ds(512, 512)
    share(z_far, out_far)
    z_copies = [
        z_copy(out_far.at[top], in_far.at[top], z_next, 0),
        z_copy(out_far.at[low], in_far.at[low], z_prev, 1),
    ]
    share(z_next, g_next)
    out_next[...] = g_next[low, :].astype(BF)
    z_copies.append(z_copy(out_next, in_next, z_next, 2))
    share(z_prev, g_prev)
    out_prev[...] = g_prev[top, :].astype(BF)
    z_copies.append(z_copy(out_prev, in_prev, z_prev, 3))
    share(z, g_own)

    l_fin.wait()
    l_fout.wait()
    for f, filt in enumerate((fin, fout)):
        for c in range(2):
            real, imag = filt[0, c], filt[1, c]
            whole = jnp.concatenate([
                jnp.concatenate([real, imag], axis=1), jnp.concatenate([-imag, real], axis=1)
            ], axis=0)
            high, low_part = split(whole)
            wk[f * 2 + c] = jnp.concatenate([high, high, low_part], axis=0)
            wl[f * 2 + c] = jnp.concatenate([high, high, low_part], axis=1)
    l_sslope.wait()
    for part in range(2):
        for c in range(2):
            spread[pl.ds(0, 512), :] = sslope[part, :, 128 * c:128 * c + 128].astype(F32)
            for kk in range(4):
                sl[c, 128 * kk:128 * kk + 128, 128 * part:128 * part + 128] = (
                    spread[pl.ds(kk, 128, stride=4), :]
                )
    l_mix.wait()
    l_unmix.wait()

    def middle(stage, c, adjoint):
        spread[...] = arrive(stage, c).reshape(1024, 128).astype(F32)
        x = jnp.concatenate([spread[pl.ds(kk, 256, stride=4), :] for kk in range(4)], axis=1)
        x = x.astype(BF)
        m = dot(mix_t[...], jnp.concatenate([x, x], axis=0))
        m = jnp.concatenate([
            jnp.concatenate([m[0:128, 128 * kk:128 * kk + 128], m[128:256, 128 * kk:128 * kk + 128]], axis=1)
            for kk in range(4)
        ], axis=0)
        if adjoint:
            m = dot_nt(left3(m), wl[2 + c])
            m = dot_nt(left3(m * sl[c]), wl[c])
        else:
            m = dot(left3(m), wk[c])
            m = dot(left3(m * sl[c]), wk[2 + c])
        m = jnp.concatenate([
            jnp.concatenate([m[128 * kk:128 * kk + 128, 128 * part:128 * part + 128] for kk in range(4)], axis=1)
            for part in range(2)
        ], axis=0)
        m = dot(unmix_t[...], right3(m))
        for kk in range(4):
            spread[pl.ds(kk, 256, stride=4), :] = m[:, 128 * kk:128 * kk + 128]
        send[stage * 2 + 2 + c] = spread[...].astype(BF).reshape(N_LAT, 32, 128)
        scatter(stage + 1, c)

    def back(stage, c, table):
        rows = arrive(stage, c).astype(F32)
        x = jnp.concatenate([rows[:, 8 * h:8 * h + 8, :].reshape(256, 128) for h in range(4)], axis=1)
        x = x.astype(BF)
        return dot(table[...], jnp.concatenate([x, x], axis=0))

    middle(0, 0, False)
    middle(0, 1, False)

    z_copies[0].wait_recv()
    z_copies[1].wait_recv()
    out_acc[top, :] = (g_next[top, :] + in_far[top, :].astype(F32)).astype(BF)
    acc_next = z_copy(out_acc.at[top], in_acc.at[top], z_next, 4)
    out_acc[low, :] = (g_prev[low, :] + in_far[low, :].astype(F32)).astype(BF)
    acc_prev = z_copy(out_acc.at[low], in_acc.at[low], z_prev, 5)
    z_copies += [acc_next, acc_prev]

    wait_for(rrecv, N_LAT - 1, s_recv.at[1])
    rsum = jnp.sum(rrecv[...], axis=0)
    rrow = jnp.concatenate([rsum[i:i + 1, :] for i in range(8)], axis=1)

    l_r.wait()
    l_p.wait()
    l_back.wait()
    own_now = jnp.sum(r[...] * r[...] / p[...], keepdims=True)[0]
    own_square = jnp.sum(d[...] * d[...], keepdims=True)[0]

    z_copies[2].wait_recv()
    z_copies[3].wait_recv()
    acc_next.wait_recv()
    acc_prev.wait_recv()
    own_weight = owz[z]
    q_top = g_own[top, :] + in_acc[top, :].astype(F32) + in_prev[...].astype(F32) + own_weight
    q_low = g_own[low, :] + in_acc[low, :].astype(F32) + in_next[...].astype(F32) + own_weight
    q[top, :] = q_top
    q[low, :] = q_low
    for h in range(4):
        high, low_part = split(q[256 * h:256 * h + 256, :])
        qcat[h] = jnp.concatenate([high, high, low_part], axis=0)

    for c in range(2):
        f = back(1, c, back_t)
        at = pl.ds(128 * c, 128)
        for h in range(4):
            rows = pl.ds(256 * h, 256)
            e = (d[h, :, at] + f[:, 128 * h:128 * h + 128]) * q[rows, at]
            if c == 0:
                esum[rows, :] = e
            else:
                esum[rows, :] = esum[rows, :] + e
    ehigh, elow = split(esum[...])
    mine = dot_nt(jnp.ones((8, 256), BF), jnp.concatenate([ehigh, elow], axis=1))
    proj[z] = mine[0:1, :]
    p_copies = [
        pltpu.make_async_remote_copy(
            proj.at[z], proj.at[z], s_send.at[2], s_recv.at[2], device_id=(me, other),
            device_id_type=MESH)
        for other in (z_next, z_prev, z_far)
    ]
    for copy in p_copies:
        copy.start()
    l_lona.wait()
    l_backa.wait()
    wait_for(proj, 3, s_recv.at[2])
    projected = (proj[0] + proj[1]) + (proj[2] + proj[3])
    gain = rrow * projected

    outs = []
    for h in range(4):
        outs.append(dot(left3(lona_t[...] * gain[:, 256 * h:256 * h + 256]), qcat[h]))
    for c in range(2):
        pack_rows(2, c, jnp.concatenate([o[:, 128 * c:128 * c + 128] for o in outs], axis=1))
        scatter(2, c)

    curve = own_square + jnp.sum(gain * projected, keepdims=True) * 0.25
    ar1[me] = jnp.where(lane == 0, own_now, jnp.where(lane == 1, curve, 0.0))
    to_all(lambda o: ar1.at[me], ar1.at[me], s_send.at[3], s_recv.at[3])

    column = jnp.transpose(jnp.broadcast_to(gain, (8, 1024)))[:, 0:1]
    for h in range(4):
        base[h] = d[h] + column[256 * h:256 * h + 256, :] * q[256 * h:256 * h + 256, :]

    wait_for(ar1, N_LAT - 1, s_recv.at[3])
    ar1z[z] = jnp.sum(ar1[...], axis=0)
    one_copies = [
        pltpu.make_async_remote_copy(
            ar1z.at[z], ar1z.at[z], s_send.at[4], s_recv.at[4], device_id=(me, other),
            device_id_type=MESH)
        for other in (z_next, z_prev, z_far)
    ]
    for copy in one_copies:
        copy.start()

    middle(2, 0, True)
    middle(2, 1, True)

    wait_for(ar1z, 3, s_recv.at[4])
    sums = (ar1z[0] + ar1z[1]) + (ar1z[2] + ar1z[3])
    norm_now, all_curve = sums[:, 0:1], sums[:, 1:2]
    alpha = norm_now / all_curve

    total = jnp.zeros((1, 1), F32)
    for c in range(2):
        f = back(3, c, backa_t)
        at = pl.ds(128 * c, 128)
        for h in range(4):
            image = base[h, :, at] + f[:, 128 * h:128 * h + 128]
            after = r[h, :, at] - alpha * image
            rn[h, :, at] = after
            total = total + jnp.sum(after * after / p[h, :, at], keepdims=True)
    out_copy = pltpu.make_async_copy(rn, rn_hbm, out_sem)
    out_copy.start()
    ar2[me] = jnp.where(lane == 0, total, 0.0)
    to_all(lambda o: ar2.at[me], ar2.at[me], s_send.at[5], s_recv.at[5])
    wait_for(ar2, N_LAT - 1, s_recv.at[5])
    ar2z[z] = jnp.sum(ar2[...], axis=0)
    two_copies = [
        pltpu.make_async_remote_copy(
            ar2z.at[z], ar2z.at[z], s_send.at[6], s_recv.at[6], device_id=(me, other),
            device_id_type=MESH)
        for other in (z_next, z_prev, z_far)
    ]
    for copy in two_copies:
        copy.start()
    wait_for(ar2z, 3, s_recv.at[6])
    norm_next = ((ar2z[0] + ar2z[1]) + (ar2z[2] + ar2z[3]))[:, 0:1]
    beta = norm_next / norm_now
    scal_ref[...] = jnp.where(lane == 0, alpha, jnp.where(lane == 1, beta, 0.0))

    for i in range(8):
        wait_for(send.at[i], N_LAT - 1, a_send.at[i])
    for copy in z_copies:
        copy.wait_send()
    wait_for(owz, 3, s_send.at[0])
    wait_for(rpart, N_LAT - 1, s_send.at[1])
    wait_for(proj, 3, s_send.at[2])
    wait_for(ar1, N_LAT - 1, s_send.at[3])
    wait_for(ar1z, 3, s_send.at[4])
    wait_for(ar2, N_LAT - 1, s_send.at[5])
    wait_for(ar2z, 3, s_send.at[6])
    out_copy.wait()


def finish(scal, state, direction, rn, precond, state_out, rn_out, direction_out):
    alpha, beta = scal[0, 0], scal[0, 1]
    now = direction[...]
    after = rn[...]
    state_out[...] = state[...] + alpha * now
    rn_out[...] = after
    direction_out[...] = after / precond[...] + beta * now


def shards(
    state, residual, direction, precond, token_slope, spectral_slope, filter_in, filter_out,
    w_up, w_down, obs_weight, obs_token, obs_count, obs_rinv,
):
    bands, width, depth = direction.shape
    tabs = make_tables(width, bands * N_LAT)
    tables = [jnp.asarray(tabs[k]) for k in ("lon", "back", "lon_adj", "back_adj", "mix", "unmix")]
    hbm = pl.BlockSpec(memory_space=pl.ANY)
    vm = pltpu.VMEM
    field = vm((4, 256, 256), F32)
    scratch = [
        field, field, field, vm((1024, 1024), BF), vm((2, 512, 256), BF),
        vm((2, 2, 128, 128), F32), vm((2, 2, 128, 128), F32), vm((1024, 1024), BF),
        vm((1024, 1024), BF), vm((1, 4, 128), jnp.int32), vm((1, 4, 128), F32),
        vm((256, 768), BF), vm((256, 512), BF), vm((256, 256), F32), vm((256, 512), BF),
        vm((256, 512), BF), vm((256, 768), BF),
        vm((4, 1, 256), F32), vm((2, 512, 256), F32), vm((4, 768, 256), BF), vm((4, 256, 768), BF),
        vm((1024, 1024), BF), vm((8, 128), F32), vm((1024, 256), F32), vm((1024, 256), F32),
        vm((1024, 256), F32), vm((1024, 256), F32), vm((4, 768, 256), BF), vm((1024, 128), F32),
        field, vm((1024, 128), F32), vm((8, 128), F32),
        vm((8, N_LAT, 32, 128), BF), vm((8, N_LAT, 32, 128), BF),
        vm((N_LAT, 8, 128), F32), vm((N_LAT, 8, 128), F32),
        vm((1024, 256), BF), vm((512, 256), BF), vm((512, 256), BF), vm((1024, 256), BF),
        vm((1024, 256), BF), vm((512, 256), BF), vm((512, 256), BF), vm((1024, 256), BF),
        vm((4, 1, 1024), F32), vm((N_LAT, 1, 128), F32), vm((4, 1, 128), F32),
        vm((N_LAT, 1, 128), F32), vm((4, 1, 128), F32), field,
        pltpu.SemaphoreType.DMA((18,)), pltpu.SemaphoreType.DMA((8,)), pltpu.SemaphoreType.DMA((8,)),
        pltpu.SemaphoreType.DMA((6,)), pltpu.SemaphoreType.DMA((6,)), pltpu.SemaphoreType.DMA((7,)),
        pltpu.SemaphoreType.DMA((7,)), pltpu.SemaphoreType.DMA,
    ]
    rn, scal = pl.pallas_call(
        kernel,
        out_shape=(
            jax.ShapeDtypeStruct((4, 256, 256), F32), jax.ShapeDtypeStruct((1, 128), F32),
        ),
        in_specs=[pl.BlockSpec(memory_space=pltpu.SMEM)] + [hbm] * 18,
        out_specs=(hbm, pl.BlockSpec(memory_space=pltpu.VMEM)),
        scratch_shapes=scratch,
        compiler_params=pltpu.CompilerParams(
            collective_id=0, has_side_effects=True, vmem_limit_bytes=56 << 20
        ),
        cost_estimate=pl.CostEstimate(flops=4 * 10**9, bytes_accessed=14 << 20, transcendentals=0),
        name="spectral_step",
    )(
        obs_count, direction, residual, precond, token_slope,
        spectral_slope.reshape(2, 512, 256), filter_in, filter_out, w_up, w_down,
        obs_weight.reshape(1, 256), obs_token, obs_rinv, *tables,
    )
    block = pl.BlockSpec((1, 256, 256), lambda i: (i, 0, 0))
    shape = jax.ShapeDtypeStruct((4, 256, 256), F32)
    return pl.pallas_call(
        finish,
        out_shape=(shape, shape, shape),
        grid=(4,),
        in_specs=[pl.BlockSpec(memory_space=pltpu.SMEM)] + [block] * 4,
        out_specs=(block, block, block),
        cost_estimate=pl.CostEstimate(flops=10**6, bytes_accessed=8 << 20, transcendentals=0),
        name="update",
    )(scal, state, direction, rn, precond)


def solution(mesh):
    return jax.shard_map(
        shards,
        mesh=mesh,
        in_specs=(
            P("lat", None, "ch"), P("lat", None, "ch"), P("lat", None, "ch"), P("lat", None, "ch"),
            P("lat", "ch"), P(None, None, "lat", "ch"), P(None, "ch", None, None),
            P(None, "ch", None, None), P(None, "ch"), P("ch", None), P("ch"),
            P("lat", None, None), P("lat", None), P("lat", None, None),
        ),
        out_specs=(P("lat", None, "ch"), P("lat", None, "ch"), P("lat", None, "ch")),
        check_vma=False,
    )
```

```python
import functools
import math

import jax
import jax.numpy as jnp
import ml_dtypes
import numpy as np
from jax import lax
from jax.experimental import pallas as pl
from jax.experimental.pallas import tpu as pltpu
from jax.sharding import PartitionSpec as P

MESH = pl.DeviceIdType.MESH
F32 = jnp.float32
BF = jnp.bfloat16
NT = (((1,), (1,)), ((), ()))
N_LAT = 32
N_CH = 4


def halves(table):
    high = table.astype(ml_dtypes.bfloat16)
    low = (table - high.astype(np.float32)).astype(ml_dtypes.bfloat16)
    return high, low


def angles(length, count):
    place = (np.arange(count)[:, None] * np.arange(length)[None, :]) % length
    angle = (2.0 * math.pi / length) * place.astype(np.float64)
    return np.cos(angle).astype(np.float32), np.sin(angle).astype(np.float32)


def make_tables(width, height):
    count = width // 2
    cos, sin = angles(width, count)
    scale = np.where(np.arange(count) == 0, 1.0, 2.0).astype(np.float32)[:, None] / width
    per = count // N_LAT

    def spectral_rows(c, s):
        both = np.stack([c.reshape(N_LAT, per, width), -s.reshape(N_LAT, per, width)], axis=1)
        return both.reshape(2 * count, width).astype(np.float32)

    plain = spectral_rows(cos, sin)
    inverse = spectral_rows(cos * scale, sin * scale)
    lat_cos, lat_sin = angles(height, height)
    mix = np.zeros((2, height, height, 2), np.float32)
    mix[0, :, :, 0] = lat_cos
    mix[0, :, :, 1] = lat_sin
    mix[1, :, :, 0] = -lat_sin
    mix[1, :, :, 1] = lat_cos
    mix = mix.reshape(2 * height, 2 * height)
    unmix = np.ascontiguousarray(mix.T) / np.float32(height)

    def left(table, parts):
        high, low = halves(np.ascontiguousarray(table))
        return np.concatenate([high, low, high][:parts], axis=1)

    return dict(
        lon=left(plain, 3),
        back=left(inverse.T, 2),
        lon_adj=inverse,
        back_adj=left(plain.T, 2),
        mix=left(mix, 2),
        unmix=left(unmix, 3),
    )


def split(x):
    high = x.astype(BF)
    return high, (x - high.astype(F32)).astype(BF)


def dot(a, b):
    return jnp.dot(a, b, preferred_element_type=F32)


def dot_nt(a, b):
    return lax.dot_general(a, b, NT, preferred_element_type=F32)


def right3(x):
    high, low = split(x)
    return jnp.concatenate([high, high, low], axis=0)


def left3(x):
    high, low = split(x)
    return jnp.concatenate([high, low, high], axis=1)


def kernel(
    count_ref, d_hbm, r_hbm, p_hbm, slope_hbm, sslope_hbm, fin_hbm, fout_hbm, wup_hbm, wdown_hbm,
    ow_hbm, tok_hbm, rinv_hbm, lon_hbm, back_hbm, lona_hbm, backa_hbm, mix_hbm, unmix_hbm,
    rn_hbm,
    d, r, p, slope, sslope, fin, fout, wup, wdown, tok, rinv, lon_t, back_t, lona_t, backa_t,
    mix_t, unmix_t, owz, sl, wk, wl, wupu, g_own, g_next, g_prev, q, qcat, esum, base,
    spread, send, recv, rpart, rrecv, out_far, out_next, out_prev, out_acc,
    in_far, in_next, in_prev, in_acc, proj, ar1, ar1z, ar2, rn, scal,
    load_sem, a_send, a_recv, z_send, z_recv, s_send, s_recv, out_sem,
):
    me = lax.axis_index("lat")
    z = lax.axis_index("ch")
    px, py, pc = me // 8, (me // 2) % 4, me % 2
    z_next, z_prev, z_far = (z + 1) % 4, (z + 3) % 4, (z + 2) % 4

    def peer(o):
        dx, dy, dc = o // 8, (o // 2) % 4, o % 2
        return ((px + dx) % 4) * 8 + ((py + dy) % 4) * 2 + (pc + dc) % 2

    loads = [
        pltpu.make_async_copy(src, dst, load_sem.at[i])
        for i, (src, dst) in enumerate([
            (d_hbm, d), (lon_hbm, lon_t), (tok_hbm, tok), (rinv_hbm, rinv), (ow_hbm, owz.at[z]),
            (wdown_hbm, wdown), (wup_hbm, wup), (slope_hbm, slope), (mix_hbm, mix_t), (fin_hbm, fin),
            (fout_hbm, fout), (sslope_hbm, sslope), (unmix_hbm, unmix_t), (back_hbm, back_t),
            (r_hbm, r), (p_hbm, p), (lona_hbm, lona_t), (backa_hbm, backa_t),
        ])
    ]
    for copy in loads[:5]:
        copy.start()
    (l_d, l_lon, l_tok, l_rinv, l_ow, l_wdown, l_wup, l_slope, l_mix, l_fin, l_fout, l_sslope,
     l_unmix, l_back, l_r, l_p, l_lona, l_backa) = loads

    barrier = pltpu.get_barrier_semaphore()

    peers = [peer(o) for o in range(1, N_LAT)]
    for other in peers:
        pl.semaphore_signal(barrier, inc=1, device_id=(other, z), device_id_type=MESH)
    for other in (z_next, z_prev, z_far):
        pl.semaphore_signal(barrier, inc=1, device_id=(me, other), device_id_type=MESH)
    for copy in loads[5:]:
        copy.start()

    def to_all(src_of, dst, send_sem, recv_sem):
        for other in peers:
            pltpu.make_async_remote_copy(
                src_of(other), dst, send_sem, recv_sem, device_id=(other, z), device_id_type=MESH
            ).start()

    def wait_for(ref, n, sem):
        part = ref.at[pl.ds(0, n)]
        pltpu.make_async_copy(part, part, sem).wait()

    def scatter(stage, c):
        i = stage * 2 + c
        recv[i, me] = send[i, me]
        to_all(lambda o: send.at[i, o], recv.at[i, me], a_send.at[i], a_recv.at[i])

    def arrive(stage, c):
        i = stage * 2 + c
        wait_for(recv.at[i], N_LAT - 1, a_recv.at[i])
        return recv[i]

    def z_copy(src, dst, other, k):
        copy = pltpu.make_async_remote_copy(
            src, dst, z_send.at[k], z_recv.at[k], device_id=(me, other), device_id_type=MESH
        )
        copy.start()
        return copy

    def pack_rows(stage, c, out):
        rows = out.reshape(N_LAT, 8, 512)
        rows = jnp.concatenate([rows[:, :, 128 * h:128 * h + 128] for h in range(4)], axis=1)
        send[stage * 2 + c] = rows.astype(BF)

    l_ow.wait()
    pl.semaphore_wait(barrier, N_LAT - 1 + N_CH - 1)

    ow_copies = [
        pltpu.make_async_remote_copy(
            owz.at[z], owz.at[z], s_send.at[0], s_recv.at[0], device_id=(me, other),
            device_id_type=MESH)
        for other in (z_next, z_prev, z_far)
    ]
    for copy in ow_copies:
        copy.start()
    l_d.wait()
    l_lon.wait()
    for c in range(2):
        x = jnp.concatenate([d[h, :, 128 * c:128 * c + 128] for h in range(4)], axis=1)
        pack_rows(0, c, dot(lon_t[...], right3(x)))
        scatter(0, c)

    l_tok.wait()
    l_rinv.wait()
    where_high, where_low = [], []
    rows_high = lax.broadcasted_iota(jnp.int32, (256, 128), 0)
    rows_low = lax.broadcasted_iota(jnp.int32, (128, 128), 0)
    lane = lax.broadcasted_iota(jnp.int32, (1, 128), 1)
    for j in range(4):
        token = tok[0, j:j + 1, :]
        live = jnp.where(lane < count_ref[0, j], rinv[0, j:j + 1, :], 0.0)
        hot = jnp.where(rows_high == (token >> 7), 1.0, 0.0).astype(BF)
        value = jnp.where(rows_low == (token & 127), live, 0.0)
        v0, rest = value.astype(BF), value - value.astype(BF).astype(F32)
        v1, v2 = split(rest)
        where_high += [hot, hot, hot]
        where_low += [v0, v1, v2]
    spread_now = dot_nt(jnp.concatenate(where_high, axis=1), jnp.concatenate(where_low, axis=1))
    rpart[...] = spread_now.reshape(N_LAT, 8, 128)

    rrecv[me] = rpart[me]
    to_all(lambda o: rpart.at[o], rrecv.at[me], s_send.at[1], s_recv.at[1])

    l_wdown.wait()
    l_wup.wait()
    l_slope.wait()
    wait_for(owz, 3, s_recv.at[0])
    weight = jnp.concatenate([owz[j] for j in range(4)], axis=1)
    w0, rest = weight.astype(BF), weight - weight.astype(BF).astype(F32)
    w1, w2 = split(rest)
    sub = lax.broadcasted_iota(jnp.int32, (8, 1024), 0)
    zero = jnp.zeros((8, 1024), F32)
    parts = jnp.where(sub == 0, w0.astype(F32), jnp.where(sub == 1, w1.astype(F32), jnp.where(
        sub == 2, w2.astype(F32), zero)))
    u = jnp.sum(dot_nt(parts.astype(BF), wdown[...]), axis=0, keepdims=True)

    def scaled(owner):
        rows = wup[pl.ds(pl.multiple_of(owner * 256, 256), 256), :]
        return (rows.astype(F32) * u).astype(BF)

    def share(k, dst, at):
        cols = wupu[k]
        dst[at, :] = dot_nt(slope[at, :], cols).astype(dst.dtype)

    top, low = pl.ds(0, 512), pl.ds(512, 512)
    z_copies = []
    wupu[0] = scaled(z_far)
    share(0, out_far, top)
    z_copies.append(z_copy(out_far.at[top], in_far.at[top], z_next, 0))
    share(0, out_far, low)
    z_copies.append(z_copy(out_far.at[low], in_far.at[low], z_prev, 1))
    wupu[1] = scaled(z_next)
    share(1, g_next, low)
    out_next[...] = g_next[low, :].astype(BF)
    z_copies.append(z_copy(out_next, in_next, z_next, 2))
    wupu[2] = scaled(z_prev)
    share(2, g_prev, top)
    out_prev[...] = g_prev[top, :].astype(BF)
    z_copies.append(z_copy(out_prev, in_prev, z_prev, 3))
    share(1, g_next, top)
    share(2, g_prev, low)

    l_fin.wait()
    l_fout.wait()
    for f, filt in enumerate((fin, fout)):
        for c in range(2):
            real, imag = filt[0, c], filt[1, c]
            whole = jnp.concatenate([
                jnp.concatenate([real, imag], axis=1), jnp.concatenate([-imag, real], axis=1)
            ], axis=0)
            high, low_part = split(whole)
            wk[f * 2 + c] = jnp.concatenate([high, high, low_part], axis=0)
            wl[f * 2 + c] = jnp.concatenate([high, high, low_part], axis=1)
    l_sslope.wait()
    for part in range(2):
        for c in range(2):
            spread[pl.ds(0, 512), :] = sslope[part, :, :, 128 * c:128 * c + 128].astype(F32).reshape(512, 128)
            for kk in range(4):
                sl[c, 128 * kk:128 * kk + 128, 128 * part:128 * part + 128] = (
                    spread[pl.ds(kk, 128, stride=4), :]
                )
    l_mix.wait()
    l_unmix.wait()

    def middle(stage, c, adjoint):
        spread[...] = arrive(stage, c).reshape(1024, 128).astype(F32)
        x = jnp.concatenate([spread[pl.ds(kk, 256, stride=4), :] for kk in range(4)], axis=1)
        x = x.astype(BF)
        m = dot(mix_t[...], jnp.concatenate([x, x], axis=0))
        m = jnp.concatenate([
            jnp.concatenate([m[0:128, 128 * kk:128 * kk + 128], m[128:256, 128 * kk:128 * kk + 128]], axis=1)
            for kk in range(4)
        ], axis=0)
        if adjoint:
            m = dot_nt(left3(m), wl[2 + c])
            m = dot_nt(left3(m * sl[c]), wl[c])
        else:
            m = dot(left3(m), wk[c])
            m = dot(left3(m * sl[c]), wk[2 + c])
        m = jnp.concatenate([
            jnp.concatenate([m[128 * kk:128 * kk + 128, 128 * part:128 * part + 128] for kk in range(4)], axis=1)
            for part in range(2)
        ], axis=0)
        m = dot(unmix_t[...], right3(m))
        for kk in range(4):
            spread[pl.ds(kk, 256, stride=4), :] = m[:, 128 * kk:128 * kk + 128]
        send[stage * 2 + 2 + c] = spread[...].astype(BF).reshape(N_LAT, 32, 128)
        scatter(stage + 1, c)

    def back(stage, c, table):
        rows = arrive(stage, c).astype(F32)
        x = jnp.concatenate([rows[:, 8 * h:8 * h + 8, :].reshape(256, 128) for h in range(4)], axis=1)
        x = x.astype(BF)
        return dot(table[...], jnp.concatenate([x, x], axis=0))

    middle(0, 0, False)
    middle(0, 1, False)
    wupu[3] = scaled(z)
    share(3, g_own, top)
    share(3, g_own, low)

    z_copies[0].wait_recv()
    z_copies[1].wait_recv()
    out_acc[top, :] = (g_next[top, :] + in_far[top, :].astype(F32)).astype(BF)
    acc_next = z_copy(out_acc.at[top], in_acc.at[top], z_next, 4)
    out_acc[low, :] = (g_prev[low, :] + in_far[low, :].astype(F32)).astype(BF)
    acc_prev = z_copy(out_acc.at[low], in_acc.at[low], z_prev, 5)
    z_copies += [acc_next, acc_prev]

    wait_for(rrecv, N_LAT - 1, s_recv.at[1])
    rsum = jnp.sum(rrecv[...], axis=0)
    rrow = jnp.concatenate([rsum[i:i + 1, :] for i in range(8)], axis=1)

    l_r.wait()
    l_p.wait()
    l_back.wait()
    p[...] = 1.0 / p[...]
    own_now = jnp.sum(r[...] * r[...] * p[...], keepdims=True)[0]
    own_square = jnp.sum(d[...] * d[...], keepdims=True)[0]

    z_copies[2].wait_recv()
    z_copies[3].wait_recv()
    acc_next.wait_recv()
    acc_prev.wait_recv()
    own_weight = owz[z]
    q_top = g_own[top, :] + in_acc[top, :].astype(F32) + in_prev[...].astype(F32) + own_weight
    q_low = g_own[low, :] + in_acc[low, :].astype(F32) + in_next[...].astype(F32) + own_weight
    q[top, :] = q_top
    q[low, :] = q_low
    for h in range(4):
        high, low_part = split(q[256 * h:256 * h + 256, :])
        qcat[h] = jnp.concatenate([high, high, low_part], axis=0)

    for c in range(2):
        f = back(1, c, back_t)
        at = pl.ds(128 * c, 128)
        for h in range(4):
            rows = pl.ds(256 * h, 256)
            e = (d[h, :, at] + f[:, 128 * h:128 * h + 128]) * q[rows, at]
            if c == 0:
                esum[rows, :] = e
            else:
                esum[rows, :] = esum[rows, :] + e
    ehigh, elow = split(esum[...])
    mine = dot_nt(jnp.ones((8, 256), BF), jnp.concatenate([ehigh, elow], axis=1))
    proj[z] = mine[0:1, :]
    p_copies = [
        pltpu.make_async_remote_copy(
            proj.at[z], proj.at[z], s_send.at[2], s_recv.at[2], device_id=(me, other),
            device_id_type=MESH)
        for other in (z_next, z_prev, z_far)
    ]
    for copy in p_copies:
        copy.start()
    l_lona.wait()
    l_backa.wait()
    wait_for(proj, 3, s_recv.at[2])
    projected = (proj[0] + proj[1]) + (proj[2] + proj[3])
    gain = rrow * projected

    outs = []
    for h in range(4):
        outs.append(dot(left3(lona_t[...] * gain[:, 256 * h:256 * h + 256]), qcat[h]))
    for c in range(2):
        pack_rows(2, c, jnp.concatenate([o[:, 128 * c:128 * c + 128] for o in outs], axis=1))
        scatter(2, c)

    curve = own_square + jnp.sum(gain * projected, keepdims=True) * 0.25
    ar1[me] = jnp.where(lane == 0, own_now, jnp.where(lane == 1, curve, 0.0))
    to_all(lambda o: ar1.at[me], ar1.at[me], s_send.at[3], s_recv.at[3])

    column = jnp.transpose(jnp.broadcast_to(gain, (8, 1024)))[:, 0:1]
    for h in range(4):
        base[h] = d[h] + column[256 * h:256 * h + 256, :] * q[256 * h:256 * h + 256, :]

    wait_for(ar1, N_LAT - 1, s_recv.at[3])
    ar1z[z] = jnp.sum(ar1[...], axis=0)
    one_copies = [
        pltpu.make_async_remote_copy(
            ar1z.at[z], ar1z.at[z], s_send.at[4], s_recv.at[4], device_id=(me, other),
            device_id_type=MESH)
        for other in (z_next, z_prev, z_far)
    ]
    for copy in one_copies:
        copy.start()

    middle(2, 0, True)
    middle(2, 1, True)

    wait_for(ar1z, 3, s_recv.at[4])
    sums = (ar1z[0] + ar1z[1]) + (ar1z[2] + ar1z[3])
    norm_now, all_curve = sums[:, 0:1], sums[:, 1:2]
    alpha = norm_now / all_curve

    total = jnp.zeros((1, 128), F32)
    for c in range(2):
        f = back(3, c, backa_t)
        at = pl.ds(128 * c, 128)
        for h in range(4):
            image = base[h, :, at] + f[:, 128 * h:128 * h + 128]
            after = r[h, :, at] - alpha * image
            rn[h, :, at] = after
            total = total + jnp.sum(after * after * p[h, :, at], axis=0, keepdims=True)
    out_copies = [
        pltpu.make_async_copy(rn.at[h], rn_hbm.at[h, pl.ds(0, 256)], out_sem.at[h]) for h in range(4)
    ]
    for copy in out_copies:
        copy.start()
    mine = me * N_CH + z
    ar2[mine] = total
    for oz in (0, 1, 2, 3):
        for other in ([me] if oz else []) + peers:
            pltpu.make_async_remote_copy(
                ar2.at[mine], ar2.at[mine], s_send.at[5], s_recv.at[5],
                device_id=(other, (z + oz) % 4), device_id_type=MESH,
            ).start()
    wait_for(ar2, N_LAT * N_CH - 1, s_recv.at[5])
    norm_next = jnp.sum(jnp.sum(ar2[...], axis=0), axis=1, keepdims=True)
    beta = norm_next / norm_now
    place = lax.broadcasted_iota(jnp.int32, (8, 256), 1)
    scal[...] = jnp.where(place == 0, alpha, jnp.where(place == 1, beta, 0.0))
    out_copies.append(pltpu.make_async_copy(scal, rn_hbm.at[0, pl.ds(256, 8)], out_sem.at[4]))
    out_copies[-1].start()

    for i in range(8):
        wait_for(send.at[i], N_LAT - 1, a_send.at[i])
    for copy in z_copies:
        copy.wait_send()
    wait_for(owz, 3, s_send.at[0])
    wait_for(rpart, N_LAT - 1, s_send.at[1])
    wait_for(proj, 3, s_send.at[2])
    wait_for(ar1, N_LAT - 1, s_send.at[3])
    wait_for(ar1z, 3, s_send.at[4])
    wait_for(ar2, N_LAT * N_CH - 1, s_send.at[5])
    for copy in out_copies:
        copy.wait()


def finish(
    state, direction, precond, rn, state_out, rn_out, direction_out,
    w_state, w_rn, w_direction, out_sem,
):
    puts = []

    def put(k, i, src, dst):
        puts.append(pltpu.make_async_copy(src.at[i], dst.at[i], out_sem.at[k, i]))
        puts[-1].start()

    alpha, beta = rn[0, 256:257, 0:1], rn[0, 256:257, 1:2]
    for i in range(4):
        now, after = direction[i], rn[i, 0:256, :]
        w_rn[i] = after
        put(0, i, w_rn, rn_out)
        w_state[i] = state[i] + alpha * now
        put(1, i, w_state, state_out)
        w_direction[i] = after / precond[i] + beta * now
        put(2, i, w_direction, direction_out)
    for copy in puts:
        copy.wait()


def shards(
    state, residual, direction, precond, token_slope, spectral_slope, filter_in, filter_out,
    w_up, w_down, obs_weight, obs_token, obs_count, obs_rinv,
):
    bands, width, depth = direction.shape
    tabs = make_tables(width, bands * N_LAT)
    tables = [jnp.asarray(tabs[k]) for k in ("lon", "back", "lon_adj", "back_adj", "mix", "unmix")]
    hbm = pl.BlockSpec(memory_space=pl.ANY)
    vm = pltpu.VMEM
    field = vm((4, 256, 256), F32)
    scratch = [
        field, field, field, vm((1024, 1024), BF), vm((2, 128, 4, 256), BF),
        vm((2, 2, 128, 128), F32), vm((2, 2, 128, 128), F32), vm((1024, 1024), BF),
        vm((1024, 1024), BF), vm((1, 4, 128), jnp.int32), vm((1, 4, 128), F32),
        vm((256, 768), BF), vm((256, 512), BF), vm((256, 256), F32), vm((256, 512), BF),
        vm((256, 512), BF), vm((256, 768), BF),
        vm((4, 1, 256), F32), vm((2, 512, 256), F32), vm((4, 768, 256), BF), vm((4, 256, 768), BF),
        vm((4, 256, 1024), BF), vm((1024, 256), F32), vm((1024, 256), F32),
        vm((1024, 256), F32), vm((1024, 256), F32), vm((4, 768, 256), BF), vm((1024, 128), F32),
        field, vm((1024, 128), F32),
        vm((8, N_LAT, 32, 128), BF), vm((8, N_LAT, 32, 128), BF),
        vm((N_LAT, 8, 128), F32), vm((N_LAT, 8, 128), F32),
        vm((1024, 256), BF), vm((512, 256), BF), vm((512, 256), BF), vm((1024, 256), BF),
        vm((1024, 256), BF), vm((512, 256), BF), vm((512, 256), BF), vm((1024, 256), BF),
        vm((4, 1, 1024), F32), vm((N_LAT, 1, 128), F32), vm((4, 1, 128), F32),
        vm((N_LAT * N_CH, 1, 128), F32), field, vm((8, 256), F32),
        pltpu.SemaphoreType.DMA((18,)), pltpu.SemaphoreType.DMA((8,)), pltpu.SemaphoreType.DMA((8,)),
        pltpu.SemaphoreType.DMA((6,)), pltpu.SemaphoreType.DMA((6,)), pltpu.SemaphoreType.DMA((6,)),
        pltpu.SemaphoreType.DMA((6,)), pltpu.SemaphoreType.DMA((5,)),
    ]
    rn = pl.pallas_call(
        kernel,
        out_shape=jax.ShapeDtypeStruct((4, 264, 256), F32),
        in_specs=[pl.BlockSpec(memory_space=pltpu.SMEM)] + [hbm] * 18,
        out_specs=hbm,
        scratch_shapes=scratch,
        compiler_params=pltpu.CompilerParams(
            collective_id=0, has_side_effects=True, vmem_limit_bytes=58 << 20
        ),
        cost_estimate=pl.CostEstimate(flops=4 * 10**9, bytes_accessed=14 << 20, transcendentals=0),
        name="spectral_step",
    )(
        obs_count, direction, residual, precond, token_slope,
        spectral_slope, filter_in, filter_out, w_up, w_down,
        obs_weight.reshape(1, 256), obs_token, obs_rinv, *tables,
    )
    shape = jax.ShapeDtypeStruct((4, 256, 256), F32)
    return pl.pallas_call(
        finish,
        out_shape=(shape, shape, shape),
        in_specs=[pl.BlockSpec(memory_space=pltpu.VMEM)] * 4,
        out_specs=(hbm, hbm, hbm),
        scratch_shapes=[field] * 3 + [pltpu.SemaphoreType.DMA((3, 4))],
        compiler_params=pltpu.CompilerParams(vmem_limit_bytes=24 << 20),
        cost_estimate=pl.CostEstimate(flops=10**6, bytes_accessed=7 << 20, transcendentals=0),
        name="update",
    )(state, direction, precond, rn)


def solution(mesh):
    return jax.shard_map(
        shards,
        mesh=mesh,
        in_specs=(
            P("lat", None, "ch"), P("lat", None, "ch"), P("lat", None, "ch"), P("lat", None, "ch"),
            P("lat", "ch"), P(None, None, "lat", "ch"), P(None, "ch", None, None),
            P(None, "ch", None, None), P(None, "ch"), P("ch", None), P("ch"),
            P("lat", None, None), P("lat", None), P("lat", None, None),
        ),
        out_specs=(P("lat", None, "ch"), P("lat", None, "ch"), P("lat", None, "ch")),
        check_vma=False,
    )
```

```python
import functools
import math

import jax
import jax.numpy as jnp
import ml_dtypes
import numpy as np
from jax import lax
from jax.experimental import pallas as pl
from jax.experimental.pallas import tpu as pltpu
from jax.sharding import PartitionSpec as P

MESH = pl.DeviceIdType.MESH
F32 = jnp.float32
BF = jnp.bfloat16
NT = (((1,), (1,)), ((), ()))
N_LAT = 32
N_CH = 4


def halves(table):
    high = table.astype(ml_dtypes.bfloat16)
    low = (table - high.astype(np.float32)).astype(ml_dtypes.bfloat16)
    return high, low


def angles(length, count):
    place = (np.arange(count)[:, None] * np.arange(length)[None, :]) % length
    angle = (2.0 * math.pi / length) * place.astype(np.float64)
    return np.cos(angle).astype(np.float32), np.sin(angle).astype(np.float32)


def make_tables(width, height):
    count = width // 2
    cos, sin = angles(width, count)
    scale = np.where(np.arange(count) == 0, 1.0, 2.0).astype(np.float32)[:, None] / width
    per = count // N_LAT

    def spectral_rows(c, s):
        both = np.stack([c.reshape(N_LAT, per, width), -s.reshape(N_LAT, per, width)], axis=1)
        return both.reshape(2 * count, width).astype(np.float32)

    plain = spectral_rows(cos, sin)
    inverse = spectral_rows(cos * scale, sin * scale)
    lat_cos, lat_sin = angles(height, height)
    mix = np.zeros((2, height, height, 2), np.float32)
    mix[0, :, :, 0] = lat_cos
    mix[0, :, :, 1] = lat_sin
    mix[1, :, :, 0] = -lat_sin
    mix[1, :, :, 1] = lat_cos
    mix = mix.reshape(2 * height, 2 * height)
    unmix = np.ascontiguousarray(mix.T) / np.float32(height)

    def left(table, parts):
        high, low = halves(np.ascontiguousarray(table))
        return np.concatenate([high, low, high][:parts], axis=1)

    return dict(
        lon=left(plain, 3),
        back=left(inverse.T, 2),
        lon_adj=inverse,
        back_adj=left(plain.T, 2),
        mix=left(mix, 2),
        unmix=left(unmix, 3),
    )


def split(x):
    high = x.astype(BF)
    return high, (x - high.astype(F32)).astype(BF)


def dot(a, b):
    return jnp.dot(a, b, preferred_element_type=F32)


def dot_nt(a, b):
    return lax.dot_general(a, b, NT, preferred_element_type=F32)


def right3(x):
    high, low = split(x)
    return jnp.concatenate([high, high, low], axis=0)


def left3(x):
    high, low = split(x)
    return jnp.concatenate([high, low, high], axis=1)


def kernel(
    count_ref, d_hbm, r_hbm, p_hbm, slope_hbm, sslope_hbm, fin_hbm, fout_hbm, wup_hbm, wdown_hbm,
    ow_hbm, tok_hbm, rinv_hbm, lon_hbm, back_hbm, lona_hbm, backa_hbm, mix_hbm, unmix_hbm,
    rn_hbm,
    d, r, p, slope, sslope, fin, fout, wup, wdown, tok, rinv, lon_t, back_t, lona_t, backa_t,
    mix_t, unmix_t, owz, sl, wk, wl, wupu, g_own, g_next, g_prev, q, qcat, base,
    spread, send, recv, rpart, rrecv, out_far, out_next, out_prev, out_acc,
    in_far, in_next, in_prev, in_acc, proj, ar1, ar1z, ar2, rn, scal,
    load_sem, a_send, a_recv, z_send, z_recv, s_send, s_recv, out_sem,
):
    me = lax.axis_index("lat")
    z = lax.axis_index("ch")
    px, py, pc = me // 8, (me // 2) % 4, me % 2
    z_next, z_prev, z_far = (z + 1) % 4, (z + 3) % 4, (z + 2) % 4

    def peer(o):
        dx, dy, dc = o // 8, (o // 2) % 4, o % 2
        return ((px + dx) % 4) * 8 + ((py + dy) % 4) * 2 + (pc + dc) % 2

    barrier = pltpu.get_barrier_semaphore()

    def hops(o):
        dx, dy, dc = o // 8, (o // 2) % 4, o % 2
        return min(dx, 4 - dx) + min(dy, 4 - dy) + dc / 4

    peers = [peer(o) for o in sorted(range(1, N_LAT), key=hops, reverse=True)]
    for other in peers:
        pl.semaphore_signal(barrier, inc=1, device_id=(other, z), device_id_type=MESH)
    for other in (z_next, z_prev, z_far):
        pl.semaphore_signal(barrier, inc=1, device_id=(me, other), device_id_type=MESH)

    loads = [
        pltpu.make_async_copy(src, dst, load_sem.at[i])
        for i, (src, dst) in enumerate([
            (d_hbm, d), (lon_hbm, lon_t), (tok_hbm, tok), (rinv_hbm, rinv), (ow_hbm, owz.at[z]),
            (wdown_hbm, wdown), (wup_hbm, wup), (slope_hbm, slope), (mix_hbm, mix_t), (fin_hbm, fin),
            (fout_hbm, fout), (sslope_hbm, sslope), (unmix_hbm, unmix_t), (back_hbm, back_t),
            (r_hbm, r), (p_hbm, p), (lona_hbm, lona_t), (backa_hbm, backa_t),
        ])
    ]
    for copy in loads[:5]:
        copy.start()
    (l_d, l_lon, l_tok, l_rinv, l_ow, l_wdown, l_wup, l_slope, l_mix, l_fin, l_fout, l_sslope,
     l_unmix, l_back, l_r, l_p, l_lona, l_backa) = loads

    for copy in loads[5:]:
        copy.start()

    def to_all(src_of, dst, send_sem, recv_sem):
        for other in peers:
            pltpu.make_async_remote_copy(
                src_of(other), dst, send_sem, recv_sem, device_id=(other, z), device_id_type=MESH
            ).start()

    def wait_for(ref, n, sem):
        part = ref.at[pl.ds(0, n)]
        pltpu.make_async_copy(part, part, sem).wait()

    def scatter(stage, c):
        i = stage * 2 + c
        recv[i, me] = send[i, me]
        to_all(lambda o: send.at[i, o], recv.at[i, me], a_send.at[i], a_recv.at[i])

    def arrive(stage, c):
        i = stage * 2 + c
        wait_for(recv.at[i], N_LAT - 1, a_recv.at[i])
        return recv[i]

    def z_copy(src, dst, other, k):
        copy = pltpu.make_async_remote_copy(
            src, dst, z_send.at[k], z_recv.at[k], device_id=(me, other), device_id_type=MESH
        )
        copy.start()
        return copy

    def pack_rows(stage, c, out):
        rows = out.reshape(N_LAT, 8, 512)
        rows = jnp.concatenate([rows[:, :, 128 * h:128 * h + 128] for h in range(4)], axis=1)
        send[stage * 2 + c] = rows.astype(BF)

    l_ow.wait()
    pl.semaphore_wait(barrier, N_LAT - 1 + N_CH - 1)

    ow_copies = [
        pltpu.make_async_remote_copy(
            owz.at[z], owz.at[z], s_send.at[0], s_recv.at[0], device_id=(me, other),
            device_id_type=MESH)
        for other in (z_next, z_prev, z_far)
    ]
    for copy in ow_copies:
        copy.start()
    l_d.wait()
    l_lon.wait()
    for c in range(2):
        x = jnp.concatenate([d[h, :, 128 * c:128 * c + 128] for h in range(4)], axis=1)
        pack_rows(0, c, dot(lon_t[...], right3(x)))
        scatter(0, c)

    l_tok.wait()
    l_rinv.wait()
    where_high, where_low = [], []
    rows_high = lax.broadcasted_iota(jnp.int32, (256, 128), 0)
    rows_low = lax.broadcasted_iota(jnp.int32, (128, 128), 0)
    lane = lax.broadcasted_iota(jnp.int32, (1, 128), 1)
    for j in range(4):
        token = tok[0, j:j + 1, :]
        live = jnp.where(lane < count_ref[0, j], rinv[0, j:j + 1, :], 0.0)
        hot = jnp.where(rows_high == (token >> 7), 1.0, 0.0).astype(BF)
        value = jnp.where(rows_low == (token & 127), live, 0.0)
        v0, rest = value.astype(BF), value - value.astype(BF).astype(F32)
        v1, v2 = split(rest)
        where_high += [hot, hot, hot]
        where_low += [v0, v1, v2]
    spread_now = dot_nt(jnp.concatenate(where_high, axis=1), jnp.concatenate(where_low, axis=1))
    rpart[...] = spread_now.reshape(N_LAT, 8, 128)

    rrecv[me] = rpart[me]
    to_all(lambda o: rpart.at[o], rrecv.at[me], s_send.at[1], s_recv.at[1])

    l_wdown.wait()
    l_wup.wait()
    l_slope.wait()
    wait_for(owz, 3, s_recv.at[0])
    weight = jnp.concatenate([owz[j] for j in range(4)], axis=1)
    w0, rest = weight.astype(BF), weight - weight.astype(BF).astype(F32)
    w1, w2 = split(rest)
    sub = lax.broadcasted_iota(jnp.int32, (8, 1024), 0)
    zero = jnp.zeros((8, 1024), F32)
    parts = jnp.where(sub == 0, w0.astype(F32), jnp.where(sub == 1, w1.astype(F32), jnp.where(
        sub == 2, w2.astype(F32), zero)))
    u = jnp.sum(dot_nt(parts.astype(BF), wdown[...]), axis=0, keepdims=True)

    def scaled(owner):
        rows = wup[pl.ds(pl.multiple_of(owner * 256, 256), 256), :]
        return (rows.astype(F32) * u).astype(BF)

    def share(k, dst, at):
        cols = wupu[k]
        dst[at, :] = dot_nt(slope[at, :], cols).astype(dst.dtype)

    top, low = pl.ds(0, 512), pl.ds(512, 512)
    z_copies = []
    wupu[0] = scaled(z_far)
    share(0, out_far, top)
    z_copies.append(z_copy(out_far.at[top], in_far.at[top], z_next, 0))
    share(0, out_far, low)
    z_copies.append(z_copy(out_far.at[low], in_far.at[low], z_prev, 1))
    wupu[1] = scaled(z_next)
    share(1, g_next, low)
    out_next[...] = g_next[low, :].astype(BF)
    z_copies.append(z_copy(out_next, in_next, z_next, 2))
    wupu[2] = scaled(z_prev)
    share(2, g_prev, top)
    out_prev[...] = g_prev[top, :].astype(BF)
    z_copies.append(z_copy(out_prev, in_prev, z_prev, 3))
    share(1, g_next, top)
    share(2, g_prev, low)

    l_fin.wait()
    l_fout.wait()
    for f, filt in enumerate((fin, fout)):
        for c in range(2):
            real, imag = filt[0, c], filt[1, c]
            whole = jnp.concatenate([
                jnp.concatenate([real, imag], axis=1), jnp.concatenate([-imag, real], axis=1)
            ], axis=0)
            high, low_part = split(whole)
            wk[f * 2 + c] = jnp.concatenate([high, high, low_part], axis=0)
            wl[f * 2 + c] = jnp.concatenate([high, high, low_part], axis=1)
    l_sslope.wait()
    for part in range(2):
        for c in range(2):
            spread[pl.ds(0, 512), :] = sslope[part, :, :, 128 * c:128 * c + 128].astype(F32).reshape(512, 128)
            for kk in range(4):
                sl[c, 128 * kk:128 * kk + 128, 128 * part:128 * part + 128] = (
                    spread[pl.ds(kk, 128, stride=4), :]
                )
    l_mix.wait()
    l_unmix.wait()

    def middle(stage, c, adjoint):
        spread[...] = arrive(stage, c).reshape(1024, 128).astype(F32)
        x = jnp.concatenate([spread[pl.ds(kk, 256, stride=4), :] for kk in range(4)], axis=1)
        x = x.astype(BF)
        m = dot(mix_t[...], jnp.concatenate([x, x], axis=0))
        m = jnp.concatenate([
            jnp.concatenate([m[0:128, 128 * kk:128 * kk + 128], m[128:256, 128 * kk:128 * kk + 128]], axis=1)
            for kk in range(4)
        ], axis=0)
        if adjoint:
            m = dot_nt(left3(m), wl[2 + c])
            m = dot_nt(left3(m * sl[c]), wl[c])
        else:
            m = dot(left3(m), wk[c])
            m = dot(left3(m * sl[c]), wk[2 + c])
        m = jnp.concatenate([
            jnp.concatenate([m[128 * kk:128 * kk + 128, 128 * part:128 * part + 128] for kk in range(4)], axis=1)
            for part in range(2)
        ], axis=0)
        m = dot(unmix_t[...], right3(m))
        for kk in range(4):
            spread[pl.ds(kk, 256, stride=4), :] = m[:, 128 * kk:128 * kk + 128]
        send[stage * 2 + 2 + c] = spread[...].astype(BF).reshape(N_LAT, 32, 128)
        scatter(stage + 1, c)

    def back(stage, c, table):
        rows = arrive(stage, c).astype(F32)
        x = jnp.concatenate([rows[:, 8 * h:8 * h + 8, :].reshape(256, 128) for h in range(4)], axis=1)
        x = x.astype(BF)
        return dot(table[...], jnp.concatenate([x, x], axis=0))

    middle(0, 0, False)
    middle(0, 1, False)

    z_copies[0].wait_recv()
    z_copies[1].wait_recv()
    out_acc[top, :] = (g_next[top, :] + in_far[top, :].astype(F32)).astype(BF)
    acc_next = z_copy(out_acc.at[top], in_acc.at[top], z_next, 4)
    out_acc[low, :] = (g_prev[low, :] + in_far[low, :].astype(F32)).astype(BF)
    acc_prev = z_copy(out_acc.at[low], in_acc.at[low], z_prev, 5)
    z_copies += [acc_next, acc_prev]
    wupu[3] = scaled(z)
    share(3, g_own, top)
    share(3, g_own, low)

    wait_for(rrecv, N_LAT - 1, s_recv.at[1])
    rsum = jnp.sum(rrecv[...], axis=0)
    rrow = jnp.concatenate([rsum[i:i + 1, :] for i in range(8)], axis=1)

    l_r.wait()
    l_p.wait()
    l_back.wait()
    p[...] = 1.0 / p[...]
    own_now = jnp.sum(r[...] * r[...] * p[...], keepdims=True)[0]
    own_square = jnp.sum(d[...] * d[...], keepdims=True)[0]

    for c in range(2):
        f = back(1, c, back_t)
        at = pl.ds(128 * c, 128)
        for h in range(4):
            base[h, :, at] = d[h, :, at] + f[:, 128 * h:128 * h + 128]

    z_copies[2].wait_recv()
    z_copies[3].wait_recv()
    acc_next.wait_recv()
    acc_prev.wait_recv()
    own_weight = owz[z]
    sums = []
    for at, direct, first in ((top, in_prev, 0), (low, in_next, 2)):
        value = g_own[at, :] + in_acc[at, :].astype(F32) + direct[...].astype(F32) + own_weight
        q[at, :] = value
        e = base[pl.ds(first, 2)].reshape(512, 256) * value
        sums.append(e[:, 0:128] + e[:, 128:256])
    ehigh, elow = split(jnp.concatenate(sums, axis=0))
    mine = dot_nt(jnp.ones((8, 256), BF), jnp.concatenate([ehigh, elow], axis=1))
    proj[z] = mine[0:1, :]
    p_copies = [
        pltpu.make_async_remote_copy(
            proj.at[z], proj.at[z], s_send.at[2], s_recv.at[2], device_id=(me, other),
            device_id_type=MESH)
        for other in (z_next, z_prev, z_far)
    ]
    for copy in p_copies:
        copy.start()
    for h in range(4):
        qcat[h] = right3(q[256 * h:256 * h + 256, :])
    l_lona.wait()
    l_backa.wait()
    wait_for(proj, 3, s_recv.at[2])
    projected = (proj[0] + proj[1]) + (proj[2] + proj[3])
    gain = rrow * projected

    outs = []
    for h in range(4):
        outs.append(dot(left3(lona_t[...] * gain[:, 256 * h:256 * h + 256]), qcat[h]))
    for c in range(2):
        pack_rows(2, c, jnp.concatenate([o[:, 128 * c:128 * c + 128] for o in outs], axis=1))
        scatter(2, c)

    curve = own_square + jnp.sum(gain * projected, keepdims=True) * 0.25
    ar1[me] = jnp.where(lane == 0, own_now, jnp.where(lane == 1, curve, 0.0))
    to_all(lambda o: ar1.at[me], ar1.at[me], s_send.at[3], s_recv.at[3])

    column = jnp.transpose(jnp.broadcast_to(gain, (8, 1024)))[:, 0:1]
    for h in range(4):
        base[h] = d[h] + column[256 * h:256 * h + 256, :] * q[256 * h:256 * h + 256, :]

    wait_for(ar1, N_LAT - 1, s_recv.at[3])
    ar1z[z] = jnp.sum(ar1[...], axis=0)
    one_copies = [
        pltpu.make_async_remote_copy(
            ar1z.at[z], ar1z.at[z], s_send.at[4], s_recv.at[4], device_id=(me, other),
            device_id_type=MESH)
        for other in (z_next, z_prev, z_far)
    ]
    for copy in one_copies:
        copy.start()

    middle(2, 0, True)
    middle(2, 1, True)

    wait_for(ar1z, 3, s_recv.at[4])
    sums = (ar1z[0] + ar1z[1]) + (ar1z[2] + ar1z[3])
    norm_now, all_curve = sums[:, 0:1], sums[:, 1:2]
    alpha = norm_now / all_curve

    total = jnp.zeros((1, 128), F32)
    for c in range(2):
        f = back(3, c, backa_t)
        at = pl.ds(128 * c, 128)
        for h in range(4):
            image = base[h, :, at] + f[:, 128 * h:128 * h + 128]
            after = r[h, :, at] - alpha * image
            rn[h, :, at] = after
            total = total + jnp.sum(after * after * p[h, :, at], axis=0, keepdims=True)
    out_copies = [
        pltpu.make_async_copy(rn.at[h], rn_hbm.at[h, pl.ds(0, 256)], out_sem.at[h]) for h in range(4)
    ]
    for copy in out_copies:
        copy.start()
    mine = me * N_CH + z
    ar2[mine] = total
    for oz in (2, 1, 3, 0):
        for other in peers + ([me] if oz else []):
            pltpu.make_async_remote_copy(
                ar2.at[mine], ar2.at[mine], s_send.at[5], s_recv.at[5],
                device_id=(other, (z + oz) % 4), device_id_type=MESH,
            ).start()
    for i in range(8):
        wait_for(send.at[i], N_LAT - 1, a_send.at[i])
    for copy in z_copies:
        copy.wait_send()
    wait_for(owz, 3, s_send.at[0])
    wait_for(rpart, N_LAT - 1, s_send.at[1])
    wait_for(proj, 3, s_send.at[2])
    wait_for(ar1, N_LAT - 1, s_send.at[3])
    wait_for(ar1z, 3, s_send.at[4])
    wait_for(ar2, N_LAT * N_CH - 1, s_recv.at[5])
    norm_next = jnp.sum(jnp.sum(ar2[...], axis=0), axis=1, keepdims=True)
    beta = norm_next / norm_now
    place = lax.broadcasted_iota(jnp.int32, (8, 256), 1)
    scal[...] = jnp.where(place == 0, alpha, jnp.where(place == 1, beta, 0.0))
    out_copies.append(pltpu.make_async_copy(scal, rn_hbm.at[0, pl.ds(256, 8)], out_sem.at[4]))
    out_copies[-1].start()

    wait_for(ar2, N_LAT * N_CH - 1, s_send.at[5])
    for copy in out_copies:
        copy.wait()


def finish(
    state, direction, precond, rn, state_out, rn_out, direction_out,
    w_state, w_rn, w_direction, out_sem,
):
    puts = []

    def put(k, i, src, dst):
        puts.append(pltpu.make_async_copy(src.at[i], dst.at[i], out_sem.at[k, i]))
        puts[-1].start()

    alpha, beta = rn[0, 256:257, 0:1], rn[0, 256:257, 1:2]
    for i in range(4):
        now, after = direction[i], rn[i, 0:256, :]
        w_rn[i] = after
        put(0, i, w_rn, rn_out)
        w_state[i] = state[i] + alpha * now
        put(1, i, w_state, state_out)
        w_direction[i] = after / precond[i] + beta * now
        put(2, i, w_direction, direction_out)
    for copy in puts:
        copy.wait()


def shards(
    state, residual, direction, precond, token_slope, spectral_slope, filter_in, filter_out,
    w_up, w_down, obs_weight, obs_token, obs_count, obs_rinv,
):
    bands, width, depth = direction.shape
    tabs = make_tables(width, bands * N_LAT)
    tables = [jnp.asarray(tabs[k]) for k in ("lon", "back", "lon_adj", "back_adj", "mix", "unmix")]
    hbm = pl.BlockSpec(memory_space=pl.ANY)
    vm = pltpu.VMEM
    field = vm((4, 256, 256), F32)
    scratch = [
        field, field, field, vm((1024, 1024), BF), vm((2, 128, 4, 256), BF),
        vm((2, 2, 128, 128), F32), vm((2, 2, 128, 128), F32), vm((1024, 1024), BF),
        vm((1024, 1024), BF), vm((1, 4, 128), jnp.int32), vm((1, 4, 128), F32),
        vm((256, 768), BF), vm((256, 512), BF), vm((256, 256), F32), vm((256, 512), BF),
        vm((256, 512), BF), vm((256, 768), BF),
        vm((4, 1, 256), F32), vm((2, 512, 256), F32), vm((4, 768, 256), BF), vm((4, 256, 768), BF),
        vm((4, 256, 1024), BF), vm((1024, 256), F32), vm((1024, 256), F32),
        vm((1024, 256), F32), vm((1024, 256), F32), vm((4, 768, 256), BF),
        field, vm((1024, 128), F32),
        vm((8, N_LAT, 32, 128), BF), vm((8, N_LAT, 32, 128), BF),
        vm((N_LAT, 8, 128), F32), vm((N_LAT, 8, 128), F32),
        vm((1024, 256), BF), vm((512, 256), BF), vm((512, 256), BF), vm((1024, 256), BF),
        vm((1024, 256), BF), vm((512, 256), BF), vm((512, 256), BF), vm((1024, 256), BF),
        vm((4, 1, 1024), F32), vm((N_LAT, 1, 128), F32), vm((4, 1, 128), F32),
        vm((N_LAT * N_CH, 1, 128), F32), field, vm((8, 256), F32),
        pltpu.SemaphoreType.DMA((18,)), pltpu.SemaphoreType.DMA((8,)), pltpu.SemaphoreType.DMA((8,)),
        pltpu.SemaphoreType.DMA((6,)), pltpu.SemaphoreType.DMA((6,)), pltpu.SemaphoreType.DMA((6,)),
        pltpu.SemaphoreType.DMA((6,)), pltpu.SemaphoreType.DMA((5,)),
    ]
    rn = pl.pallas_call(
        kernel,
        out_shape=jax.ShapeDtypeStruct((4, 264, 256), F32),
        in_specs=[pl.BlockSpec(memory_space=pltpu.SMEM)] + [hbm] * 18,
        out_specs=hbm,
        scratch_shapes=scratch,
        compiler_params=pltpu.CompilerParams(
            collective_id=0, has_side_effects=True, vmem_limit_bytes=58 << 20
        ),
        cost_estimate=pl.CostEstimate(flops=4 * 10**9, bytes_accessed=14 << 20, transcendentals=0),
        name="spectral_step",
    )(
        obs_count, direction, residual, precond, token_slope,
        spectral_slope, filter_in, filter_out, w_up, w_down,
        obs_weight.reshape(1, 256), obs_token, obs_rinv, *tables,
    )
    shape = jax.ShapeDtypeStruct((4, 256, 256), F32)
    return pl.pallas_call(
        finish,
        out_shape=(shape, shape, shape),
        in_specs=[pl.BlockSpec(memory_space=pltpu.VMEM)] * 4,
        out_specs=(hbm, hbm, hbm),
        scratch_shapes=[field] * 3 + [pltpu.SemaphoreType.DMA((3, 4))],
        compiler_params=pltpu.CompilerParams(vmem_limit_bytes=24 << 20),
        cost_estimate=pl.CostEstimate(flops=10**6, bytes_accessed=7 << 20, transcendentals=0),
        name="update",
    )(state, direction, precond, rn)


def solution(mesh):
    return jax.shard_map(
        shards,
        mesh=mesh,
        in_specs=(
            P("lat", None, "ch"), P("lat", None, "ch"), P("lat", None, "ch"), P("lat", None, "ch"),
            P("lat", "ch"), P(None, None, "lat", "ch"), P(None, "ch", None, None),
            P(None, "ch", None, None), P(None, "ch"), P("ch", None), P("ch"),
            P("lat", None, None), P("lat", None), P("lat", None, None),
        ),
        out_specs=(P("lat", None, "ch"), P("lat", None, "ch"), P("lat", None, "ch")),
        check_vma=False,
    )
```

```python
import functools
import math

import jax
import jax.numpy as jnp
import ml_dtypes
import numpy as np
from jax import lax
from jax.experimental import pallas as pl
from jax.experimental.pallas import tpu as pltpu
from jax.sharding import PartitionSpec as P

MESH = pl.DeviceIdType.MESH
F32 = jnp.float32
BF = jnp.bfloat16
NT = (((1,), (1,)), ((), ()))
N_LAT = 32
N_CH = 4


def halves(table):
    high = table.astype(ml_dtypes.bfloat16)
    low = (table - high.astype(np.float32)).astype(ml_dtypes.bfloat16)
    return high, low


def angles(length, count):
    place = (np.arange(count)[:, None] * np.arange(length)[None, :]) % length
    angle = (2.0 * math.pi / length) * place.astype(np.float64)
    return np.cos(angle).astype(np.float32), np.sin(angle).astype(np.float32)


def make_tables(width, height):
    count = width // 2
    cos, sin = angles(width, count)
    scale = np.where(np.arange(count) == 0, 1.0, 2.0).astype(np.float32)[:, None] / width
    per = count // N_LAT

    def spectral_rows(c, s):
        both = np.stack([c.reshape(N_LAT, per, width), -s.reshape(N_LAT, per, width)], axis=1)
        return both.reshape(2 * count, width).astype(np.float32)

    plain = spectral_rows(cos, sin)
    inverse = spectral_rows(cos * scale, sin * scale)
    lat_cos, lat_sin = angles(height, height)
    mix = np.zeros((2, height, height, 2), np.float32)
    mix[0, :, :, 0] = lat_cos
    mix[0, :, :, 1] = lat_sin
    mix[1, :, :, 0] = -lat_sin
    mix[1, :, :, 1] = lat_cos
    mix = mix.reshape(2 * height, 2 * height)
    unmix = np.ascontiguousarray(mix.T) / np.float32(height)

    def left(table, parts):
        high, low = halves(np.ascontiguousarray(table))
        return np.concatenate([high, low, high][:parts], axis=1)

    return dict(
        lon=left(plain, 3),
        back=left(inverse.T, 2),
        lon_adj=inverse,
        back_adj=left(plain.T, 2),
        mix=left(mix, 2),
        unmix=left(unmix, 3),
    )


def split(x):
    high = x.astype(BF)
    return high, (x - high.astype(F32)).astype(BF)


def dot(a, b):
    return jnp.dot(a, b, preferred_element_type=F32)


def dot_nt(a, b):
    return lax.dot_general(a, b, NT, preferred_element_type=F32)


def right3(x):
    high, low = split(x)
    return jnp.concatenate([high, high, low], axis=0)


def left3(x):
    high, low = split(x)
    return jnp.concatenate([high, low, high], axis=1)


def kernel(
    count_ref, d_hbm, r_hbm, p_hbm, slope_hbm, sslope_hbm, fin_hbm, fout_hbm, wup_hbm, wdown_hbm,
    ow_hbm, tok_hbm, rinv_hbm, lon_hbm, back_hbm, lona_hbm, backa_hbm, mix_hbm, unmix_hbm,
    rn_hbm,
    d, r, p, slope, sslope, fin, fout, wup, wdown, tok, rinv, lon_t, back_t, lona_t, backa_t,
    mix_t, unmix_t, owz, sl, wk, wl, wupu, g_own, g_next, g_prev, q, qcat, base,
    spread, send, recv, rpart, rrecv, out_far, out_next, out_prev, out_acc,
    in_far, in_next, in_prev, in_acc, proj, ar1, ar1z, ar2, rn, scal,
    load_sem, a_send, a_recv, z_send, z_recv, s_send, s_recv, out_sem,
):
    me = lax.axis_index("lat")
    z = lax.axis_index("ch")
    px, py, pc = me // 8, (me // 2) % 4, me % 2
    z_next, z_prev, z_far = (z + 1) % 4, (z + 3) % 4, (z + 2) % 4

    def peer(o):
        dx, dy, dc = o // 8, (o // 2) % 4, o % 2
        return ((px + dx) % 4) * 8 + ((py + dy) % 4) * 2 + (pc + dc) % 2

    barrier = pltpu.get_barrier_semaphore()

    def hops(o):
        dx, dy, dc = o // 8, (o // 2) % 4, o % 2
        return min(dx, 4 - dx) + min(dy, 4 - dy) + dc / 4

    peers = [peer(o) for o in sorted(range(1, N_LAT), key=hops, reverse=True)]
    for other in peers:
        pl.semaphore_signal(barrier, inc=1, device_id=(other, z), device_id_type=MESH)
    for other in (z_next, z_prev, z_far):
        pl.semaphore_signal(barrier, inc=1, device_id=(me, other), device_id_type=MESH)

    loads = [
        pltpu.make_async_copy(src, dst, load_sem.at[i])
        for i, (src, dst) in enumerate([
            (d_hbm, d), (lon_hbm, lon_t), (tok_hbm, tok), (rinv_hbm, rinv), (ow_hbm, owz.at[z]),
            (wdown_hbm, wdown), (wup_hbm, wup), (slope_hbm, slope), (mix_hbm, mix_t), (fin_hbm, fin),
            (fout_hbm, fout), (sslope_hbm, sslope), (unmix_hbm, unmix_t), (back_hbm, back_t),
            (r_hbm, r), (p_hbm, p), (lona_hbm, lona_t), (backa_hbm, backa_t),
        ])
    ]
    for copy in loads[:5]:
        copy.start()
    (l_d, l_lon, l_tok, l_rinv, l_ow, l_wdown, l_wup, l_slope, l_mix, l_fin, l_fout, l_sslope,
     l_unmix, l_back, l_r, l_p, l_lona, l_backa) = loads

    for copy in loads[5:]:
        copy.start()

    def to_all(src_of, dst, send_sem, recv_sem):
        for other in peers:
            pltpu.make_async_remote_copy(
                src_of(other), dst, send_sem, recv_sem, device_id=(other, z), device_id_type=MESH
            ).start()

    def wait_for(ref, n, sem):
        part = ref.at[pl.ds(0, n)]
        pltpu.make_async_copy(part, part, sem).wait()

    def scatter(stage, c):
        i = stage * 2 + c
        recv[i, me] = send[i, me]
        to_all(lambda o: send.at[i, o], recv.at[i, me], a_send.at[i], a_recv.at[i])

    def arrive(stage, c):
        i = stage * 2 + c
        wait_for(recv.at[i], N_LAT - 1, a_recv.at[i])
        return recv[i]

    def z_copy(src, dst, other, k):
        copy = pltpu.make_async_remote_copy(
            src, dst, z_send.at[k], z_recv.at[k], device_id=(me, other), device_id_type=MESH
        )
        copy.start()
        return copy

    def pack_rows(stage, c, out):
        rows = out.reshape(N_LAT, 8, 512)
        rows = jnp.concatenate([rows[:, :, 128 * h:128 * h + 128] for h in range(4)], axis=1)
        send[stage * 2 + c] = rows.astype(BF)

    l_ow.wait()
    pl.semaphore_wait(barrier, N_LAT - 1 + N_CH - 1)

    ow_copies = [
        pltpu.make_async_remote_copy(
            owz.at[z], owz.at[z], s_send.at[0], s_recv.at[0], device_id=(me, other),
            device_id_type=MESH)
        for other in (z_next, z_prev, z_far)
    ]
    for copy in ow_copies:
        copy.start()
    l_d.wait()
    l_lon.wait()
    for c in range(2):
        x = jnp.concatenate([d[h, :, 128 * c:128 * c + 128] for h in range(4)], axis=1)
        pack_rows(0, c, dot(lon_t[...], right3(x)))
        scatter(0, c)

    l_tok.wait()
    l_rinv.wait()
    where_high, where_low = [], []
    rows_high = lax.broadcasted_iota(jnp.int32, (256, 128), 0)
    rows_low = lax.broadcasted_iota(jnp.int32, (128, 128), 0)
    lane = lax.broadcasted_iota(jnp.int32, (1, 128), 1)
    for j in range(4):
        token = tok[0, j:j + 1, :]
        live = jnp.where(lane < count_ref[0, j], rinv[0, j:j + 1, :], 0.0)
        hot = jnp.where(rows_high == (token >> 7), 1.0, 0.0).astype(BF)
        value = jnp.where(rows_low == (token & 127), live, 0.0)
        v0, rest = value.astype(BF), value - value.astype(BF).astype(F32)
        v1, v2 = split(rest)
        where_high += [hot, hot, hot]
        where_low += [v0, v1, v2]
    spread_now = dot_nt(jnp.concatenate(where_high, axis=1), jnp.concatenate(where_low, axis=1))
    rpart[...] = spread_now.reshape(N_LAT, 8, 128)

    rrecv[me] = rpart[me]
    to_all(lambda o: rpart.at[o], rrecv.at[me], s_send.at[1], s_recv.at[1])

    l_wdown.wait()
    l_wup.wait()
    l_slope.wait()
    wait_for(owz, 3, s_recv.at[0])
    weight = jnp.concatenate([owz[j] for j in range(4)], axis=1)
    w0, rest = weight.astype(BF), weight - weight.astype(BF).astype(F32)
    w1, w2 = split(rest)
    sub = lax.broadcasted_iota(jnp.int32, (8, 1024), 0)
    zero = jnp.zeros((8, 1024), F32)
    parts = jnp.where(sub == 0, w0.astype(F32), jnp.where(sub == 1, w1.astype(F32), jnp.where(
        sub == 2, w2.astype(F32), zero)))
    u = jnp.sum(dot_nt(parts.astype(BF), wdown[...]), axis=0, keepdims=True)

    def scaled(owner):
        rows = wup[pl.ds(pl.multiple_of(owner * 256, 256), 256), :]
        return (rows.astype(F32) * u).astype(BF)

    def share(k, dst, at):
        cols = wupu[k]
        dst[at, :] = dot_nt(slope[at, :], cols).astype(dst.dtype)

    top, low = pl.ds(0, 512), pl.ds(512, 512)
    z_copies = []
    wupu[0] = scaled(z_far)
    share(0, out_far, top)
    z_copies.append(z_copy(out_far.at[top], in_far.at[top], z_next, 0))
    share(0, out_far, low)
    z_copies.append(z_copy(out_far.at[low], in_far.at[low], z_prev, 1))
    wupu[1] = scaled(z_next)
    share(1, g_next, low)
    out_next[...] = g_next[low, :].astype(BF)
    z_copies.append(z_copy(out_next, in_next, z_next, 2))
    wupu[2] = scaled(z_prev)
    share(2, g_prev, top)
    out_prev[...] = g_prev[top, :].astype(BF)
    z_copies.append(z_copy(out_prev, in_prev, z_prev, 3))
    share(1, g_next, top)
    share(2, g_prev, low)

    l_fin.wait()
    l_fout.wait()
    for f, filt in enumerate((fin, fout)):
        for c in range(2):
            real, imag = filt[0, c], filt[1, c]
            whole = jnp.concatenate([
                jnp.concatenate([real, imag], axis=1), jnp.concatenate([-imag, real], axis=1)
            ], axis=0)
            high, low_part = split(whole)
            wk[f * 2 + c] = jnp.concatenate([high, high, low_part], axis=0)
            wl[f * 2 + c] = jnp.concatenate([high, high, low_part], axis=1)
    l_sslope.wait()
    for part in range(2):
        for c in range(2):
            spread[pl.ds(0, 512), :] = sslope[part, :, :, 128 * c:128 * c + 128].astype(F32).reshape(512, 128)
            for kk in range(4):
                sl[c, 128 * kk:128 * kk + 128, 128 * part:128 * part + 128] = (
                    spread[pl.ds(kk, 128, stride=4), :]
                )
    l_mix.wait()
    l_unmix.wait()

    def middle(stage, c, adjoint):
        spread[...] = arrive(stage, c).reshape(1024, 128).astype(F32)
        x = jnp.concatenate([spread[pl.ds(kk, 256, stride=4), :] for kk in range(4)], axis=1)
        x = x.astype(BF)
        m = dot(mix_t[...], jnp.concatenate([x, x], axis=0))
        m = jnp.concatenate([
            jnp.concatenate([m[0:128, 128 * kk:128 * kk + 128], m[128:256, 128 * kk:128 * kk + 128]], axis=1)
            for kk in range(4)
        ], axis=0)
        if adjoint:
            m = dot_nt(left3(m), wl[2 + c])
            m = dot_nt(left3(m * sl[c]), wl[c])
        else:
            m = dot(left3(m), wk[c])
            m = dot(left3(m * sl[c]), wk[2 + c])
        m = jnp.concatenate([
            jnp.concatenate([m[128 * kk:128 * kk + 128, 128 * part:128 * part + 128] for kk in range(4)], axis=1)
            for part in range(2)
        ], axis=0)
        m = dot(unmix_t[...], right3(m))
        for kk in range(4):
            spread[pl.ds(kk, 256, stride=4), :] = m[:, 128 * kk:128 * kk + 128]
        send[stage * 2 + 2 + c] = spread[...].astype(BF).reshape(N_LAT, 32, 128)
        scatter(stage + 1, c)

    def back(stage, c, table):
        rows = arrive(stage, c).astype(F32)
        x = jnp.concatenate([rows[:, 8 * h:8 * h + 8, :].reshape(256, 128) for h in range(4)], axis=1)
        x = x.astype(BF)
        return dot(table[...], jnp.concatenate([x, x], axis=0))

    middle(0, 0, False)
    middle(0, 1, False)

    z_copies[0].wait_recv()
    z_copies[1].wait_recv()
    out_acc[top, :] = (g_next[top, :] + in_far[top, :].astype(F32)).astype(BF)
    acc_next = z_copy(out_acc.at[top], in_acc.at[top], z_next, 4)
    out_acc[low, :] = (g_prev[low, :] + in_far[low, :].astype(F32)).astype(BF)
    acc_prev = z_copy(out_acc.at[low], in_acc.at[low], z_prev, 5)
    z_copies += [acc_next, acc_prev]
    wupu[3] = scaled(z)
    share(3, g_own, top)
    share(3, g_own, low)

    wait_for(rrecv, N_LAT - 1, s_recv.at[1])
    rsum = jnp.sum(rrecv[...], axis=0)
    rrow = jnp.concatenate([rsum[i:i + 1, :] for i in range(8)], axis=1)

    l_r.wait()
    l_p.wait()
    l_back.wait()
    p[...] = 1.0 / p[...]
    own_now = jnp.sum(r[...] * r[...] * p[...], keepdims=True)[0]
    own_square = jnp.sum(d[...] * d[...], keepdims=True)[0]

    for c in range(2):
        f = back(1, c, back_t)
        at = pl.ds(128 * c, 128)
        for h in range(4):
            base[h, :, at] = d[h, :, at] + f[:, 128 * h:128 * h + 128]

    z_copies[2].wait_recv()
    z_copies[3].wait_recv()
    acc_next.wait_recv()
    acc_prev.wait_recv()
    own_weight = owz[z]
    sums = []
    for at, direct, first in ((top, in_prev, 0), (low, in_next, 2)):
        value = g_own[at, :] + in_acc[at, :].astype(F32) + direct[...].astype(F32) + own_weight
        q[at, :] = value
        e = base[pl.ds(first, 2)].reshape(512, 256) * value
        sums.append(e[:, 0:128] + e[:, 128:256])
    ehigh, elow = split(jnp.concatenate(sums, axis=0))
    mine = dot_nt(jnp.ones((8, 256), BF), jnp.concatenate([ehigh, elow], axis=1))
    proj[z] = mine[0:1, :]
    p_copies = [
        pltpu.make_async_remote_copy(
            proj.at[z], proj.at[z], s_send.at[2], s_recv.at[2], device_id=(me, other),
            device_id_type=MESH)
        for other in (z_next, z_prev, z_far)
    ]
    for copy in p_copies:
        copy.start()
    for h in range(4):
        qcat[h] = right3(q[256 * h:256 * h + 256, :])
    l_lona.wait()
    l_backa.wait()
    wait_for(proj, 3, s_recv.at[2])
    projected = (proj[0] + proj[1]) + (proj[2] + proj[3])
    gain = rrow * projected

    outs = []
    for h in range(4):
        outs.append(dot(left3(lona_t[...] * gain[:, 256 * h:256 * h + 256]), qcat[h]))
    for c in range(2):
        pack_rows(2, c, jnp.concatenate([o[:, 128 * c:128 * c + 128] for o in outs], axis=1))
        scatter(2, c)

    curve = own_square + jnp.sum(gain * projected, keepdims=True) * 0.25
    ar1[me] = jnp.where(lane == 0, own_now, jnp.where(lane == 1, curve, 0.0))
    to_all(lambda o: ar1.at[me], ar1.at[me], s_send.at[3], s_recv.at[3])

    column = jnp.transpose(jnp.broadcast_to(gain, (8, 1024)))[:, 0:1]
    for h in range(4):
        base[h] = d[h] + column[256 * h:256 * h + 256, :] * q[256 * h:256 * h + 256, :]

    wait_for(ar1, N_LAT - 1, s_recv.at[3])
    ar1z[z] = jnp.sum(ar1[...], axis=0)
    one_copies = [
        pltpu.make_async_remote_copy(
            ar1z.at[z], ar1z.at[z], s_send.at[4], s_recv.at[4], device_id=(me, other),
            device_id_type=MESH)
        for other in (z_next, z_prev, z_far)
    ]
    for copy in one_copies:
        copy.start()

    middle(2, 0, True)
    middle(2, 1, True)

    wait_for(ar1z, 3, s_recv.at[4])
    sums = (ar1z[0] + ar1z[1]) + (ar1z[2] + ar1z[3])
    norm_now, all_curve = sums[:, 0:1], sums[:, 1:2]
    alpha = norm_now / all_curve

    total = jnp.zeros((1, 128), F32)
    for c in range(2):
        f = back(3, c, backa_t)
        at = pl.ds(128 * c, 128)
        for h in range(4):
            image = base[h, :, at] + f[:, 128 * h:128 * h + 128]
            after = r[h, :, at] - alpha * image
            rn[h, :, at] = after
            total = total + jnp.sum(after * after * p[h, :, at], axis=0, keepdims=True)
    out_copies = [
        pltpu.make_async_copy(rn.at[h], rn_hbm.at[h, pl.ds(0, 256)], out_sem.at[h]) for h in range(4)
    ]
    for copy in out_copies:
        copy.start()
    mine = me * N_CH + z
    ar2[mine] = total
    for oz in (2, 1, 3, 0):
        for other in peers + ([me] if oz else []):
            pltpu.make_async_remote_copy(
                ar2.at[mine], ar2.at[mine], s_send.at[5], s_recv.at[5],
                device_id=(other, (z + oz) % 4), device_id_type=MESH,
            ).start()
    for i in range(8):
        wait_for(send.at[i], N_LAT - 1, a_send.at[i])
    for copy in z_copies:
        copy.wait_send()
    wait_for(owz, 3, s_send.at[0])
    wait_for(rpart, N_LAT - 1, s_send.at[1])
    wait_for(proj, 3, s_send.at[2])
    wait_for(ar1, N_LAT - 1, s_send.at[3])
    wait_for(ar1z, 3, s_send.at[4])
    wait_for(ar2, N_LAT * N_CH - 1, s_recv.at[5])
    norm_next = jnp.sum(jnp.sum(ar2[...], axis=0), axis=1, keepdims=True)
    beta = norm_next / norm_now
    place = lax.broadcasted_iota(jnp.int32, (8, 256), 1)
    scal[...] = jnp.where(place == 0, alpha, jnp.where(place == 1, beta, 0.0))
    out_copies.append(pltpu.make_async_copy(scal, rn_hbm.at[0, pl.ds(256, 8)], out_sem.at[4]))
    out_copies[-1].start()

    wait_for(ar2, N_LAT * N_CH - 1, s_send.at[5])
    for copy in out_copies:
        copy.wait()


def finish(
    state, direction, precond, rn_hbm, state_out, rn_out, direction_out,
    rn, scal, w_state, w_direction, in_sem, out_sem,
):
    gets = [pltpu.make_async_copy(rn_hbm.at[0, pl.ds(256, 8)], scal, in_sem.at[4])]
    gets += [
        pltpu.make_async_copy(rn_hbm.at[i, pl.ds(0, 256)], rn.at[i], in_sem.at[i]) for i in range(4)
    ]
    for copy in gets:
        copy.start()
    puts = []

    def put(k, i, src, dst):
        puts.append(pltpu.make_async_copy(src.at[i], dst.at[i], out_sem.at[k, i]))
        puts[-1].start()

    gets[0].wait()
    alpha, beta = scal[0:1, 0:1], scal[0:1, 1:2]
    for i in range(4):
        w_state[i] = state[i] + alpha * direction[i]
        put(0, i, w_state, state_out)
    for i in range(4):
        gets[1 + i].wait()
        put(1, i, rn, rn_out)
        w_direction[i] = rn[i] / precond[i] + beta * direction[i]
        put(2, i, w_direction, direction_out)
    for copy in puts:
        copy.wait()


def shards(
    state, residual, direction, precond, token_slope, spectral_slope, filter_in, filter_out,
    w_up, w_down, obs_weight, obs_token, obs_count, obs_rinv,
):
    bands, width, depth = direction.shape
    tabs = make_tables(width, bands * N_LAT)
    tables = [jnp.asarray(tabs[k]) for k in ("lon", "back", "lon_adj", "back_adj", "mix", "unmix")]
    hbm = pl.BlockSpec(memory_space=pl.ANY)
    vm = pltpu.VMEM
    field = vm((4, 256, 256), F32)
    scratch = [
        field, field, field, vm((1024, 1024), BF), vm((2, 128, 4, 256), BF),
        vm((2, 2, 128, 128), F32), vm((2, 2, 128, 128), F32), vm((1024, 1024), BF),
        vm((1024, 1024), BF), vm((1, 4, 128), jnp.int32), vm((1, 4, 128), F32),
        vm((256, 768), BF), vm((256, 512), BF), vm((256, 256), F32), vm((256, 512), BF),
        vm((256, 512), BF), vm((256, 768), BF),
        vm((4, 1, 256), F32), vm((2, 512, 256), F32), vm((4, 768, 256), BF), vm((4, 256, 768), BF),
        vm((4, 256, 1024), BF), vm((1024, 256), F32), vm((1024, 256), F32),
        vm((1024, 256), F32), vm((1024, 256), F32), vm((4, 768, 256), BF),
        field, vm((1024, 128), F32),
        vm((8, N_LAT, 32, 128), BF), vm((8, N_LAT, 32, 128), BF),
        vm((N_LAT, 8, 128), F32), vm((N_LAT, 8, 128), F32),
        vm((1024, 256), BF), vm((512, 256), BF), vm((512, 256), BF), vm((1024, 256), BF),
        vm((1024, 256), BF), vm((512, 256), BF), vm((512, 256), BF), vm((1024, 256), BF),
        vm((4, 1, 1024), F32), vm((N_LAT, 1, 128), F32), vm((4, 1, 128), F32),
        vm((N_LAT * N_CH, 1, 128), F32), field, vm((8, 256), F32),
        pltpu.SemaphoreType.DMA((18,)), pltpu.SemaphoreType.DMA((8,)), pltpu.SemaphoreType.DMA((8,)),
        pltpu.SemaphoreType.DMA((6,)), pltpu.SemaphoreType.DMA((6,)), pltpu.SemaphoreType.DMA((6,)),
        pltpu.SemaphoreType.DMA((6,)), pltpu.SemaphoreType.DMA((5,)),
    ]
    rn = pl.pallas_call(
        kernel,
        out_shape=jax.ShapeDtypeStruct((112, 264, 256), F32),
        in_specs=[pl.BlockSpec(memory_space=pltpu.SMEM)] + [hbm] * 18,
        out_specs=hbm,
        scratch_shapes=scratch,
        compiler_params=pltpu.CompilerParams(
            collective_id=0, has_side_effects=True, vmem_limit_bytes=58 << 20
        ),
        cost_estimate=pl.CostEstimate(flops=4 * 10**9, bytes_accessed=14 << 20, transcendentals=0),
        name="spectral_step",
    )(
        obs_count, direction, residual, precond, token_slope,
        spectral_slope, filter_in, filter_out, w_up, w_down,
        obs_weight.reshape(1, 256), obs_token, obs_rinv, *tables,
    )
    shape = jax.ShapeDtypeStruct((4, 256, 256), F32)
    return pl.pallas_call(
        finish,
        out_shape=(shape, shape, shape),
        in_specs=[pl.BlockSpec(memory_space=pltpu.VMEM)] * 3 + [hbm],
        out_specs=(hbm, hbm, hbm),
        scratch_shapes=[field, vm((8, 256), F32), field, field] + [
            pltpu.SemaphoreType.DMA((5,)), pltpu.SemaphoreType.DMA((3, 4)),
        ],
        compiler_params=pltpu.CompilerParams(vmem_limit_bytes=40 << 20),
        cost_estimate=pl.CostEstimate(flops=10**6, bytes_accessed=7 << 20, transcendentals=0),
        name="update",
    )(state, direction, precond, rn)


def solution(mesh):
    return jax.shard_map(
        shards,
        mesh=mesh,
        in_specs=(
            P("lat", None, "ch"), P("lat", None, "ch"), P("lat", None, "ch"), P("lat", None, "ch"),
            P("lat", "ch"), P(None, None, "lat", "ch"), P(None, "ch", None, None),
            P(None, "ch", None, None), P(None, "ch"), P("ch", None), P("ch"),
            P("lat", None, None), P("lat", None), P("lat", None, None),
        ),
        out_specs=(P("lat", None, "ch"), P("lat", None, "ch"), P("lat", None, "ch")),
        check_vma=False,
    )
```
